32 devices in a mesh: fsdp: 8 (over z, x), seq: 4 (over y, core).
Axes of the slice: x: 2, y: 2, z: 4, core: 2. Of those that a mesh axis runs over, the one named last changes fastest.
Arguments:
- block_in: float32 [8, 512, 768], P('fsdp', 'seq'), may hold values from -6 to 6
- expert_ids: int32 [8, 512, 2], P('fsdp', 'seq'), may hold values from 0 to 31, all different within a row; in each aligned block of 128 rows (0 to 127, 128 to 255, ..., all dimensions but the last counted through in order) at most 10 rows name the same one
- ln1_gain: bfloat16 [768], P(('fsdp', 'seq')), may hold values from 0.5 to 1.5
- ln1_bias: bfloat16 [768], P(('fsdp', 'seq')), may hold values from -1.796875 to 1.796875
- w_query: bfloat16 [768, 768], P(('fsdp', 'seq')), may hold values from -3 to 3
- w_key: bfloat16 [768, 768], P(('fsdp', 'seq')), may hold values from -3 to 3
- w_value: bfloat16 [768, 768], P(('fsdp', 'seq')), may hold values from -0.21875 to 0.21875
- w_output: bfloat16 [768, 768], P(('fsdp', 'seq')), may hold values from -6 to 6
- ln2_gain: bfloat16 [768], P(('fsdp', 'seq')), may hold values from 0.5 to 1.5
- ln2_bias: bfloat16 [768], P(('fsdp', 'seq')), may hold values from -1.796875 to 1.796875
- w_router: bfloat16 [768, 32], P(('fsdp', 'seq')), may hold values from -8 to 8
- w_expert_in: bfloat16 [64, 768, 1536], P('fsdp', None, 'seq'), may hold values from -0.21875 to 0.21875
- w_expert_out: bfloat16 [64, 1536, 768], P('fsdp', 'seq'), may hold values from -3 to 3
- cotangent: float32 [8, 512, 768], P('fsdp', 'seq'), may hold values from -6 to 6
Outputs:
- block_out: float32 [8, 512, 768], P('fsdp', 'seq')
- grad_in: float32 [8, 512, 768], P('fsdp', 'seq')
- grad_ln1_gain: float32 [768], P(('fsdp', 'seq'))
- grad_ln1_bias: float32 [768], P(('fsdp', 'seq'))
- grad_query: float32 [768, 768], P('fsdp', 'seq')
- grad_key: float32 [768, 768], P('fsdp', 'seq')
- grad_value: float32 [768, 768], P('fsdp', 'seq')
- grad_output: float32 [768, 768], P('seq', 'fsdp')
- grad_ln2_gain: float32 [768], P(('fsdp', 'seq'))
- grad_ln2_bias: float32 [768], P(('fsdp', 'seq'))
- grad_router: float32 [768, 32], P(('fsdp', 'seq'))
- grad_expert_in: float32 [64, 768, 1536], P('fsdp', None, 'seq')
- grad_expert_out: float32 [64, 1536, 768], P('fsdp', 'seq')
The draws below stay inside these ranges and needn't reach their ends.
Inputs may be any that keep to these rules, and one draw needn't show every extreme that they name: `expert_ids`: each token names 2 different experts. Among the 128 tokens of one device (one aligned block), no expert is named more than 10 times.
All inputs are finite; a program needn't handle non-finite values.
Results may differ from the reference program's by a relative error of at most 0.025.
Values may be sent and summed in bfloat16 or wider, within the bound.
No kernel may reach another device: no remote copies, remote signals or barrier semaphores. Data moves between devices by JAX's collectives and lax.ppermute only.
A program may use at most 192 MiB of HBM per device.

```python
import math
import jax
import jax.numpy as jnp
import numpy as np
from jax import lax

D = 768
HEADS = 12
HEAD_DIM = 64
FF = 3072
EXPERTS = 32
TOP = 2
TOK_DEV = 128
SEQ_LEN = 512
IMAGES = 8
CAP = 10
HALF_FF = 1536
SLICES = 64
N_FSDP = 8
N_SEQ = 4


def bounded_normal(key, shape, spread, limit):
    return jnp.clip(jax.random.normal(key, shape, jnp.float32) * spread, -limit, limit)


def draw_w_query(key, part):
    spread = D ** (-0.5)
    return bounded_normal(jax.random.fold_in(key, 101), (D, D), spread, 3.0).astype(jnp.bfloat16)


def draw_w_key(key, part):
    spread = D ** (-0.5)
    return bounded_normal(jax.random.fold_in(key, 202), (D, D), spread, 3.0).astype(jnp.bfloat16)


def draw_w_router(key, part):
    spread = 2.0 * D ** (-0.5)
    return bounded_normal(jax.random.fold_in(key, 303), (D, EXPERTS), spread, 8.0).astype(jnp.bfloat16)


def spiked(entries, key, source, target, blocks, factor):
    owner, partner = [(jnp.arange(entries.shape[position]) // (entries.shape[position] // blocks)).reshape([-1 if axis == position else 1 for axis in range(entries.ndim)]) for position in (source, target)]
    chosen = jax.random.permutation(key, blocks)[partner]
    strong = (owner == chosen) | (owner == (partner + blocks // 2) % blocks)
    return jnp.where(strong, factor * entries, entries)


def shard_levels(own_key, shape, shards, smallest, high):
    def one(axis_at, shards_of):
        steps = jax.random.uniform(jax.random.fold_in(jax.random.fold_in(own_key, 6), axis_at), (shards_of,), jnp.float32, smallest / len(shards), high / len(shards))
        return jnp.repeat(jnp.exp(steps), shape[axis_at] // shards_of).reshape((-1,) + (1,) * (len(shape) - axis_at - 1))

    level = one(*shards[0])
    for cut in shards[1:]:
        level = level * one(*cut)
    return level


def shared_out(stream_key, own, number, rows, amount, top, bound, skew):
    order = jax.random.permutation(stream_key, amount)
    packed, ordinary = load_shares(amount, rows * top, bound, skew, True), load_shares(amount, rows * top, bound, skew, False)
    places = jnp.arange(amount)

    def named(tallies, turn):
        used = int((tallies > 0).sum())
        fixed = max(1, used // 4)
        moved = fixed + (places - fixed + turn * (used - fixed)) % max(1, amount - fixed)
        return jnp.zeros((amount,), jnp.int32).at[order[jnp.where(places < fixed, places, moved)]].set(jnp.asarray(tallies, jnp.int32))

    tallies = jnp.where(number % 4 == 0, named(packed, number // 4), named(ordinary, number - number // 4 - 1))
    mixed = jax.random.permutation(jax.random.fold_in(own, 3), amount)
    source_of, receiver = mixed[0:amount // 2 * 2:2], mixed[1:amount // 2 * 2:2]
    margin = jnp.minimum(tallies[source_of] - 1, bound - tallies[receiver]) // 2
    margin = jnp.where((source_of == order[0]) | (receiver == order[0]) | (tallies[receiver] == 0), 0, jnp.maximum(margin, 0))
    moved = jax.random.randint(jax.random.fold_in(own, 4), (amount // 2,), 0, 1 << 20) % (margin + 1)
    tallies = tallies.at[source_of].add(-moved).at[receiver].add(moved)
    members = jnp.searchsorted(jnp.cumsum(tallies), jnp.arange(rows * top), side="right").astype(jnp.int32)
    grid = members.reshape(top, rows).T
    grid = grid[jax.random.permutation(jax.random.fold_in(own, 1), rows)]
    turn = jax.random.randint(jax.random.fold_in(own, 2), (rows, 1), 0, top)
    return jnp.take_along_axis(grid, (jnp.arange(top)[None, :] + turn) % top, axis=1)


def load_shares(number_of, total, most, skew, full):
    weights = [(1 << 20) // math.isqrt(standing ** skew) + 1 for standing in range(1, number_of + 1)]
    largest = most if full else min(most, max(-(-total // number_of), total * weights[0] // sum(weights)))
    least = 1 if total - largest >= number_of - 1 else 0
    given, spare = [largest] + [least] * (number_of - 1), total - largest - least * (number_of - 1)
    while spare > 0:
        free = [i for i in range(1, number_of) if given[i] < largest] or [i for i in range(1, number_of) if given[i] < most]
        whole, remaining = sum([weights[i] for i in free]), spare
        for i in free:
            addition = min(most - given[i], max(1, remaining * weights[i] // whole), spare)
            given[i] = given[i] + addition
            spare = spare - addition
    return np.array(given)


def centred(own_key, shape, scale, most, cuts=(), held_as=jnp.bfloat16):
    entries = scale * jax.random.normal(own_key, shape, jnp.float32)
    if cuts:
        entries = entries * shard_levels(own_key, shape, cuts, -0.22, 0.18)
    return jnp.clip(entries, -most, most).astype(held_as)


def bell_draw_with(rng, dims, scale, most, pieces, heavy, held_as=jnp.bfloat16):
    values = scale * jax.random.normal(rng, dims, jnp.float32)
    if pieces:
        values = values * shard_levels(rng, dims, pieces, -0.22, 0.18)
    return jnp.clip(spiked(values, jax.random.fold_in(rng, 3), *heavy), -most, most).astype(held_as)


def setup_inputs(seed: int = 0) -> dict:
    arg_keys = jax.random.split(jax.random.key(seed), 15)
    block_in = centred(arg_keys[0], (IMAGES, SEQ_LEN, D), 1.0, 6.0, ((0, 8), (1, 4)), jnp.float32)
    expert_ids_keys = jax.random.split(jax.random.fold_in(arg_keys[1], 1), IMAGES * SEQ_LEN // TOK_DEV)
    expert_ids_turns = jax.random.permutation(jax.random.fold_in(arg_keys[1], 3), IMAGES * SEQ_LEN // TOK_DEV)
    expert_ids = jax.vmap(lambda own, number: shared_out(jax.random.fold_in(arg_keys[1], 2), own, number, TOK_DEV, EXPERTS, TOP, CAP, 2))(expert_ids_keys, expert_ids_turns).reshape((IMAGES, SEQ_LEN, TOP))
    ln1_gain = jnp.clip(1.0 + 0.1 * jax.random.normal(arg_keys[2], (D,), jnp.float32), 0.5, 1.5).astype(jnp.bfloat16)
    ln1_bias = centred(arg_keys[3], (D,), 0.3, 1.796875, ((0, 32),))
    w_query = draw_w_query(jax.random.fold_in(arg_keys[14], 71), 0)
    w_key = draw_w_key(jax.random.fold_in(arg_keys[14], 71), 0)
    w_value = centred(arg_keys[6], (D, D), D ** -0.5, 0.21875, ((0, 32),))
    w_output = centred(arg_keys[7], (D, D), (max(1, D // 512)) ** -0.5, 6.0, ((0, 32),))
    ln2_gain = jnp.clip(1.0 + 0.1 * jax.random.normal(arg_keys[8], (D,), jnp.float32), 0.5, 1.5).astype(jnp.bfloat16)
    ln2_bias = centred(arg_keys[9], (D,), 0.3, 1.796875, ((0, 32),))
    w_router = draw_w_router(jax.random.fold_in(arg_keys[14], 71), 0)
    w_expert_in = centred(arg_keys[11], (SLICES, D, HALF_FF), D ** -0.5, 0.21875, ((0, 8), (2, 4)))
    w_expert_out = centred(arg_keys[12], (SLICES, HALF_FF, D), (max(1, FF // 768)) ** -0.5, 3.0, ((0, 8), (1, 4)))
    cotangent = bell_draw_with(arg_keys[13], (IMAGES, SEQ_LEN, D), 1.0, 6.0, ((0, 8), (1, 4)), (0, 2, 8, 2.0), jnp.float32)
    return dict(block_in=block_in, expert_ids=expert_ids, ln1_gain=ln1_gain, ln1_bias=ln1_bias, w_query=w_query, w_key=w_key, w_value=w_value, w_output=w_output, ln2_gain=ln2_gain, ln2_bias=ln2_bias, w_router=w_router, w_expert_in=w_expert_in, w_expert_out=w_expert_out, cotangent=cotangent)


EPS = 1e-06
TANH_SCALE = 0.7978845608028654
CUBIC = 0.044715
HIGHEST = lax.Precision.HIGHEST

def rounded(values):
    return lax.optimization_barrier(values.astype(jnp.bfloat16)).astype(jnp.float32)

def matmul(left_side, right_side):
    return jnp.dot(left_side, right_side, preferred_element_type=jnp.float32)

def norm_forward(values):
    centre = values - lax.optimization_barrier(jnp.mean(values, -1, keepdims=True))
    inverse = lax.rsqrt(lax.optimization_barrier(jnp.mean(centre * centre, -1, keepdims=True)) + EPS)
    return (centre * inverse, inverse)

def norm_backward(grad_normed, normed, inverse):
    return inverse * (grad_normed - lax.optimization_barrier(jnp.mean(grad_normed, -1, keepdims=True)) - normed * lax.optimization_barrier(jnp.mean(grad_normed * normed, -1, keepdims=True)))

def gelu_value(inner_act):
    bent = jnp.tanh(TANH_SCALE * (inner_act + CUBIC * inner_act * inner_act * inner_act))
    return 0.5 * inner_act * (1.0 + bent)

def gelu_slope(inner_act):
    square = inner_act * inner_act
    bent = jnp.tanh(TANH_SCALE * inner_act * (1.0 + CUBIC * square))
    return 0.5 * (1.0 + bent) + 0.5 * inner_act * (1.0 - bent * bent) * TANH_SCALE * (1.0 + 3.0 * CUBIC * square)

def split_heads(matrix):
    return matrix.astype(jnp.float32).reshape(matrix.shape[0], HEADS, HEAD_DIM)

def attend(query_rows, key_rows, value_rows):
    scaling = HEAD_DIM ** (-0.5)
    scores = jnp.einsum('qhd,khd->hqk', split_heads(query_rows), split_heads(key_rows), precision=HIGHEST) * scaling
    highest = lax.optimization_barrier(jnp.max(scores, -1, keepdims=True))
    logsum = highest + jnp.log(lax.optimization_barrier(jnp.sum(jnp.exp(scores - highest), -1, keepdims=True)))
    weights = rounded(jnp.exp(scores - logsum))
    attn_mixed = jnp.einsum('hqk,khd->qhd', weights, split_heads(value_rows), precision=HIGHEST)
    return (attn_mixed.reshape(query_rows.shape[0], D).astype(jnp.bfloat16), logsum)

def attend_back(query_rows, key_rows, value_rows, attn_mixed, logsum, grad_mixed):
    scaling = HEAD_DIM ** (-0.5)
    query_heads = split_heads(query_rows)
    key_heads = split_heads(key_rows)
    scores = jnp.einsum('qhd,khd->hqk', query_heads, key_heads, precision=HIGHEST) * scaling
    attn_probs = jnp.exp(scores - logsum)
    weights = rounded(attn_probs)
    grad_heads = split_heads(grad_mixed)
    grad_values = jnp.einsum('hqk,qhd->khd', weights, grad_heads, precision=HIGHEST)
    grad_probs = jnp.einsum('qhd,khd->hqk', grad_heads, split_heads(value_rows), precision=HIGHEST)
    row_delta = lax.optimization_barrier(jnp.sum(grad_heads * split_heads(attn_mixed), -1)).T[:, :, None]
    grad_scores = rounded(attn_probs * (grad_probs - row_delta) * scaling)
    grad_queries = jnp.einsum('hqk,khd->qhd', grad_scores, key_heads, precision=HIGHEST)
    grad_keys = jnp.einsum('hqk,qhd->khd', grad_scores, query_heads, precision=HIGHEST)
    length = query_rows.shape[0]
    return (grad_queries.reshape(length, D).astype(jnp.bfloat16), grad_keys.reshape(length, D).astype(jnp.bfloat16), grad_values.reshape(length, D).astype(jnp.bfloat16))

def reference(block_in, expert_ids, ln1_gain, ln1_bias, w_query, w_key, w_value, w_output, ln2_gain, ln2_bias, w_router, w_expert_in, w_expert_out, cotangent):
    gain_one = ln1_gain.astype(jnp.float32)
    bias_one = ln1_bias.astype(jnp.float32)
    gain_two = ln2_gain.astype(jnp.float32)
    bias_two = ln2_bias.astype(jnp.float32)

    def attention_image(tokens_in):
        normed, inverse = norm_forward(tokens_in)
        normed_in = (normed * gain_one + bias_one).astype(jnp.bfloat16)
        query_rows = matmul(normed_in, w_query).astype(jnp.bfloat16)
        key_rows = matmul(normed_in, w_key).astype(jnp.bfloat16)
        value_rows = matmul(normed_in, w_value).astype(jnp.bfloat16)
        attn_mixed, logsum = attend(query_rows, key_rows, value_rows)
        return (normed_in, query_rows, key_rows, value_rows, attn_mixed, logsum, tokens_in + matmul(attn_mixed, w_output))
    kept = lax.map(attention_image, block_in)
    after_attn = kept[6]
    tokens_total = IMAGES * SEQ_LEN
    residual = after_attn.reshape(tokens_total, D)
    normed_two, inverse_two = norm_forward(residual)
    expert_rows = (normed_two * gain_two + bias_two).astype(jnp.bfloat16)
    router_probs = jax.nn.softmax(matmul(expert_rows, w_router), -1)
    chosen = expert_ids.reshape(tokens_total, TOP)
    gate_values = jnp.take_along_axis(router_probs, chosen, 1)
    route_expert = chosen.reshape(-1)
    route_gate = gate_values.reshape(-1)
    route_order = jnp.argsort(route_expert, stable=True).astype(jnp.int32)
    counts = lax.optimization_barrier(jnp.sum((route_expert[None, :] == jnp.arange(EXPERTS)[:, None]).astype(jnp.int32), 1))
    starts = (jnp.cumsum(counts) - counts).astype(jnp.int32)
    row_bound = N_FSDP * N_SEQ * CAP
    padded_order = jnp.concatenate([route_order, jnp.zeros((row_bound,), jnp.int32)])
    grad_flat = cotangent.reshape(tokens_total, D)
    weights_in = w_expert_in.reshape(EXPERTS, 2, D, HALF_FF)
    weights_out = w_expert_out.reshape(EXPERTS, 2, HALF_FF, D)

    def expert_step(carried, inputs):
        moe_sum, grad_rows, grad_gates = carried
        weight_in, weight_out, start_row, count_rows = inputs
        routes = lax.dynamic_slice_in_dim(padded_order, start_row, row_bound)
        live_rows = jnp.arange(row_bound) < count_rows
        token_index = routes // TOP
        slot_rows = jnp.where(live_rows[:, None], expert_rows[token_index], jnp.zeros((), jnp.bfloat16))
        slot_gate = jnp.where(live_rows, route_gate[routes], 0.0)
        upstream = grad_flat[token_index]
        inner_list = []
        hidden_list = []
        output = jnp.zeros((row_bound, D), jnp.float32)
        for half_index in range(2):
            inner_act = matmul(slot_rows, weight_in[half_index])
            hidden_act = gelu_value(inner_act).astype(jnp.bfloat16)
            output = output + rounded(matmul(hidden_act, weight_out[half_index]))
            inner_list.append(inner_act)
            hidden_list.append(hidden_act)
        grad_route = (slot_gate[:, None] * upstream).astype(jnp.bfloat16)
        grad_in_rows = jnp.zeros((row_bound, D), jnp.float32)
        grads_in = []
        grads_out = []
        for half_index in range(2):
            grad_hidden = matmul(grad_route, weight_out[half_index].T)
            grad_inner = (grad_hidden * gelu_slope(inner_list[half_index])).astype(jnp.bfloat16)
            grads_in.append(matmul(slot_rows.T, grad_inner))
            grads_out.append(matmul(hidden_list[half_index].T, grad_route))
            grad_in_rows = grad_in_rows + rounded(matmul(grad_inner, weight_in[half_index].T))
        moe_sum = moe_sum.at[token_index].add(slot_gate[:, None] * output)
        grad_rows = grad_rows.at[token_index].add(grad_in_rows)
        grad_gates = grad_gates.at[routes].add(jnp.where(live_rows, lax.optimization_barrier(jnp.sum(upstream * output, -1)), 0.0))
        return ((moe_sum, grad_rows, grad_gates), (jnp.stack(grads_in), jnp.stack(grads_out)))
    initial = (jnp.zeros((tokens_total, D), jnp.float32), jnp.zeros((tokens_total, D), jnp.float32), jnp.zeros((tokens_total * TOP,), jnp.float32))
    carried, stacked = lax.scan(expert_step, initial, (weights_in, weights_out, starts, counts))
    moe_sum, grad_rows, grad_gates = carried
    grad_expert_in = stacked[0].reshape(SLICES, D, HALF_FF)
    grad_expert_out = stacked[1].reshape(SLICES, HALF_FF, D)
    block_out = (residual + moe_sum).reshape(IMAGES, SEQ_LEN, D)
    grad_gate = grad_gates.reshape(tokens_total, TOP)
    onehot = (chosen[:, :, None] == jnp.arange(EXPERTS)[None, None, :]).astype(jnp.float32)
    grad_probs = lax.optimization_barrier(jnp.sum(onehot * grad_gate[:, :, None], 1))
    grad_logits = router_probs * (grad_probs - lax.optimization_barrier(jnp.sum(router_probs * grad_probs, -1, keepdims=True)))
    grad_logits_half = grad_logits.astype(jnp.bfloat16)
    grad_router = matmul(expert_rows.T, grad_logits_half)
    grad_normed_rows = grad_rows + matmul(grad_logits_half, w_router.T)
    grad_gain_two = lax.optimization_barrier(jnp.sum(grad_normed_rows * normed_two, 0))
    grad_bias_two = lax.optimization_barrier(jnp.sum(grad_normed_rows, 0))
    grad_residual = grad_flat + norm_backward(grad_normed_rows * gain_two, normed_two, inverse_two)
    grad_residual = grad_residual.reshape(IMAGES, SEQ_LEN, D)

    def attention_back(carried_sums, inputs):
        tokens_in, kept_normed, kept_query, kept_keys, kept_values, kept_mixed, kept_logsum, grad_res = inputs
        grad_res_half = grad_res.astype(jnp.bfloat16)
        grad_wo = matmul(kept_mixed.T, grad_res_half)
        grad_mixed = matmul(grad_res_half, w_output.T).astype(jnp.bfloat16)
        grad_queries, grad_keys, grad_values = attend_back(kept_query, kept_keys, kept_values, kept_mixed, kept_logsum, grad_mixed)
        grad_wq = matmul(kept_normed.T, grad_queries)
        grad_wk = matmul(kept_normed.T, grad_keys)
        grad_wv = matmul(kept_normed.T, grad_values)
        grad_normed = matmul(grad_queries, w_query.T) + matmul(grad_keys, w_key.T) + matmul(grad_values, w_value.T)
        normed, inverse = norm_forward(tokens_in)
        grad_tokens = grad_res + norm_backward(grad_normed * gain_one, normed, inverse)
        grad_terms = (grad_wq, grad_wk, grad_wv, grad_wo, lax.optimization_barrier(jnp.sum(grad_normed * normed, 0)), lax.optimization_barrier(jnp.sum(grad_normed, 0)))
        return (jax.tree.map(jnp.add, carried_sums, grad_terms), grad_tokens)
    zero_square = jnp.zeros((D, D), jnp.float32)
    zero_vector = jnp.zeros((D,), jnp.float32)
    sums_init = (zero_square, zero_square, zero_square, zero_square, zero_vector, zero_vector)
    grad_sums, grad_in = lax.scan(attention_back, sums_init, (block_in, kept[0], kept[1], kept[2], kept[3], kept[4], kept[5], grad_residual))
    return (block_out, grad_in, grad_sums[4], grad_sums[5], grad_sums[0], grad_sums[1], grad_sums[2], grad_sums[3], grad_gain_two, grad_bias_two, grad_router, grad_expert_in, grad_expert_out)
```

```python
import jax
import jax.numpy as jnp
from jax import lax
from jax.sharding import PartitionSpec as P

D = 768
HEAD_DIM = 64
EXPERTS = 32
TOP = 2
CAP = 10


EPS = 1e-06
TANH_SCALE = 0.7978845608028654
CUBIC = 0.044715


def matmul(left_side, right_side):
    return jnp.dot(left_side, right_side, preferred_element_type=jnp.float32)


def norm_forward(values):
    centre = values - jnp.mean(values, -1, keepdims=True)
    inverse = lax.rsqrt(jnp.mean(centre * centre, -1, keepdims=True) + EPS)
    return (centre * inverse, inverse)


def norm_backward(grad_normed, normed, inverse):
    return inverse * (
        grad_normed
        - jnp.mean(grad_normed, -1, keepdims=True)
        - normed * jnp.mean(grad_normed * normed, -1, keepdims=True)
    )


def gelu_both(inner_act):
    square = inner_act * inner_act
    bent = jnp.tanh(TANH_SCALE * inner_act * (1.0 + CUBIC * square))
    value = 0.5 * inner_act * (1.0 + bent)
    slope = 0.5 * (1.0 + bent) + 0.5 * inner_act * (1.0 - bent * bent) * TANH_SCALE * (
        1.0 + 3.0 * CUBIC * square
    )
    return (value, slope)


def head_view(matrix):
    return matrix.reshape(matrix.shape[0], -1, HEAD_DIM)


def attend(query_rows, key_rows, value_rows):
    scaling = HEAD_DIM ** (-0.5)
    scores = (
        jnp.einsum(
            "qhd,khd->hqk",
            head_view(query_rows),
            head_view(key_rows),
            preferred_element_type=jnp.float32,
        )
        * scaling
    )
    highest = jnp.max(scores, -1, keepdims=True)
    logsum = highest + jnp.log(jnp.sum(jnp.exp(scores - highest), -1, keepdims=True))
    weights = jnp.exp(scores - logsum).astype(jnp.bfloat16)
    attn_mixed = jnp.einsum(
        "hqk,khd->qhd", weights, head_view(value_rows), preferred_element_type=jnp.float32
    )
    return (attn_mixed.astype(jnp.bfloat16).reshape(query_rows.shape[0], -1), logsum)


def attend_back(query_rows, key_rows, value_rows, attn_mixed, logsum, grad_mixed):
    scaling = HEAD_DIM ** (-0.5)
    query_heads = head_view(query_rows)
    key_heads = head_view(key_rows)
    scores = (
        jnp.einsum("qhd,khd->hqk", query_heads, key_heads, preferred_element_type=jnp.float32)
        * scaling
    )
    attn_probs = jnp.exp(scores - logsum)
    weights = attn_probs.astype(jnp.bfloat16)
    grad_heads = head_view(grad_mixed)
    grad_values = jnp.einsum(
        "hqk,qhd->khd", weights, grad_heads, preferred_element_type=jnp.float32
    )
    grad_probs = jnp.einsum(
        "qhd,khd->hqk", grad_heads, head_view(value_rows), preferred_element_type=jnp.float32
    )
    row_delta = jnp.sum(
        grad_heads.astype(jnp.float32) * head_view(attn_mixed).astype(jnp.float32), -1
    ).T[:, :, None]
    grad_scores = (attn_probs * (grad_probs - row_delta) * scaling).astype(jnp.bfloat16)
    grad_queries = jnp.einsum(
        "hqk,khd->qhd", grad_scores, key_heads, preferred_element_type=jnp.float32
    )
    grad_keys = jnp.einsum(
        "hqk,qhd->khd", grad_scores, query_heads, preferred_element_type=jnp.float32
    )
    length = query_rows.shape[0]
    return (
        grad_queries.astype(jnp.bfloat16).reshape(length, -1),
        grad_keys.astype(jnp.bfloat16).reshape(length, -1),
        grad_values.astype(jnp.bfloat16).reshape(length, -1),
    )


FAR = [(index, index ^ 2) for index in range(4)]
NEAR = [(index, index ^ 1) for index in range(4)]


def seq_gather(block):
    pair = jnp.stack([block, lax.ppermute(block, "seq", FAR)])
    return jnp.concatenate([pair, lax.ppermute(pair, "seq", NEAR)])


def seq_reduce(partial):
    near = lax.ppermute(partial[2:], "seq", NEAR)
    pair = partial[:2].astype(jnp.float32) + near.astype(jnp.float32)
    far = lax.ppermute(pair[1].astype(jnp.bfloat16), "seq", FAR)
    return pair[0] + far.astype(jnp.float32)


def body(
    block_in,
    expert_ids,
    ln1_gain,
    ln1_bias,
    w_query,
    w_key,
    w_value,
    w_output,
    ln2_gain,
    ln2_bias,
    w_router,
    w_expert_in,
    w_expert_out,
    cotangent,
):
    bf16 = jnp.bfloat16
    f32 = jnp.float32
    fsdp_size = lax.axis_size("fsdp")
    seq_size = lax.axis_size("seq")
    devices = fsdp_size * seq_size
    shard = w_query.shape[0]
    head_cols = D // seq_size
    local_slices = w_expert_in.shape[0]
    local_experts = max(1, local_slices // 2)
    halves = local_slices // local_experts
    copies = 2 // halves
    tokens_in = block_in[0]
    upstream = cotangent[0]
    chosen = expert_ids[0]
    token_count = chosen.shape[0]

    projections = jnp.stack([w_query, w_key, w_value], 1).reshape(shard, 3, seq_size, head_cols)
    projections = projections.transpose(2, 0, 1, 3).reshape(seq_size, shard, 3 * head_cols)
    small = jnp.concatenate(
        [w_router] + [v[:, None] for v in (ln1_gain, ln1_bias, ln2_gain, ln2_bias)], 1
    )
    sent = jnp.concatenate(
        [projections, jnp.broadcast_to(small, (seq_size,) + small.shape)], 2
    )
    sent = jnp.broadcast_to(sent, (fsdp_size,) + sent.shape).reshape(devices, shard, -1)
    held = lax.all_to_all(sent, ("fsdp", "seq"), split_axis=0, concat_axis=0, tiled=True)
    held = held.reshape(D, -1)
    w_heads = held[:, : 3 * head_cols]
    full_router = held[:, 3 * head_cols : 3 * head_cols + EXPERTS]
    vectors = held[:, 3 * head_cols + EXPERTS :].T.astype(f32)
    gain_one, bias_one, gain_two, bias_two = (vectors[0], vectors[1], vectors[2], vectors[3])
    moves = [
        (fsdp_size * part + place, seq_size * place + part)
        for part in range(seq_size)
        for place in range(fsdp_size)
    ]
    w_out_rows = lax.all_to_all(
        jnp.broadcast_to(
            lax.ppermute(w_output, ("fsdp", "seq"), moves), (fsdp_size,) + w_output.shape
        ),
        "fsdp",
        split_axis=0,
        concat_axis=0,
        tiled=True,
    ).reshape(head_cols, D)

    hot = (chosen.reshape(-1)[:, None] == jnp.arange(EXPERTS)[None, :]).astype(bf16)
    routes = token_count * TOP
    before = (jnp.arange(routes)[:, None] > jnp.arange(routes)[None, :]).astype(bf16)
    slot = jnp.sum(matmul(before, hot) * hot.astype(f32), 1).astype(jnp.int32)
    position = (chosen.reshape(-1) * CAP + slot).reshape(token_count, TOP)
    place = jnp.arange(EXPERTS * CAP)
    picks = []
    for choice in range(TOP):
        pick = (place[:, None] == position[:, choice][None, :]).astype(bf16)
        pick = jnp.broadcast_to(
            pick.reshape(EXPERTS, 1, CAP, token_count), (EXPERTS, copies, CAP, token_count)
        )
        picks.append(pick.reshape(EXPERTS * copies * CAP, token_count))
    pick_any = picks[0] + picks[1]

    def to_experts(rows):
        table = matmul(pick_any, rows).astype(bf16).reshape(fsdp_size, local_experts * CAP, D)
        received = lax.all_to_all(table, "fsdp", split_axis=0, concat_axis=0, tiled=True)
        received = received.reshape(fsdp_size, local_experts, CAP, D).transpose(1, 0, 2, 3)
        gathered = seq_gather(received)
        return gathered.transpose(1, 0, 2, 3, 4).reshape(local_experts, -1, D)

    def from_experts(partial):
        partial = partial.astype(bf16).reshape(local_experts, seq_size, fsdp_size, CAP, D)
        partial = partial.transpose(1, 2, 0, 3, 4).reshape(
            seq_size, fsdp_size, local_experts * CAP, D
        )
        summed = seq_reduce(partial).astype(bf16)
        returned = lax.all_to_all(summed, "fsdp", split_axis=0, concat_axis=0, tiled=True)
        return returned.reshape(-1, D)

    all_tokens = seq_gather(tokens_in).reshape(-1, D)
    all_normed, all_inverse = norm_forward(all_tokens)
    all_normed_in = (all_normed * gain_one + bias_one).astype(bf16)
    qkv = matmul(all_normed_in, w_heads).astype(bf16)
    query_rows, key_rows, value_rows = (
        qkv[:, :head_cols],
        qkv[:, head_cols : 2 * head_cols],
        qkv[:, 2 * head_cols :],
    )
    head_mixed, logsum = attend(query_rows, key_rows, value_rows)
    out_partial = matmul(head_mixed, w_out_rows).astype(bf16)
    residual = tokens_in + seq_reduce(out_partial.reshape(seq_size, token_count, D))

    normed_two, inverse_two = norm_forward(residual)
    expert_rows = (normed_two * gain_two + bias_two).astype(bf16)
    router_probs = jax.nn.softmax(matmul(expert_rows, full_router), -1)
    onehot = (chosen[:, :, None] == jnp.arange(EXPERTS)[None, None, :]).astype(f32)
    gate_values = jnp.sum(onehot * router_probs[:, None, :], -1)
    slot_rows = to_experts(expert_rows)
    slot_cots = to_experts(upstream.astype(bf16))

    first = lax.axis_index("fsdp") * local_slices // 2
    wanted = first + jnp.arange(local_experts)
    slot_probs = jax.nn.softmax(matmul(slot_rows, full_router), -1)
    slot_gates = jnp.sum(
        jnp.where(jnp.arange(EXPERTS) == wanted[:, None, None], slot_probs, 0.0),
        -1,
        keepdims=True,
    )
    hidden_cols = w_expert_in.shape[2]
    expert_in = w_expert_in.reshape(local_experts, halves, D, hidden_cols)
    expert_out = w_expert_out.reshape(local_experts, halves, hidden_cols, D)
    inner_act = jnp.einsum("erd,ekdf->ekrf", slot_rows, expert_in, preferred_element_type=f32)
    value, slope = gelu_both(inner_act)
    hidden_act = value.astype(bf16)
    route_partial = jnp.einsum(
        "ekrf,ekfd->erd", hidden_act, expert_out, preferred_element_type=f32
    )
    slot_grads = (slot_gates * slot_cots.astype(f32)).astype(bf16)
    grad_hidden = jnp.einsum("erd,ekfd->ekrf", slot_grads, expert_out, preferred_element_type=f32)
    grad_inner = (grad_hidden * slope).astype(bf16)
    grad_partial = jnp.einsum(
        "ekrf,ekdf->erd", grad_inner, expert_in, preferred_element_type=f32
    )
    out_table = from_experts(route_partial)
    grad_table = from_experts(grad_partial)
    grad_expert_in = jnp.einsum(
        "erd,ekrf->ekdf", slot_rows, grad_inner, preferred_element_type=f32
    ).reshape(w_expert_in.shape)
    grad_expert_out = jnp.einsum(
        "ekrf,erd->ekfd", hidden_act, slot_grads, preferred_element_type=f32
    ).reshape(w_expert_out.shape)

    picked = [matmul(pick.T, out_table) for pick in picks]
    block_out = residual + gate_values[:, :1] * picked[0] + gate_values[:, 1:] * picked[1]
    grad_gate = jnp.stack([jnp.sum(upstream * part, -1) for part in picked], 1)
    grad_probs = jnp.sum(onehot * grad_gate[:, :, None], 1)
    grad_logits = router_probs * (
        grad_probs - jnp.sum(router_probs * grad_probs, -1, keepdims=True)
    )
    grad_logits_half = grad_logits.astype(bf16)
    grad_router = matmul(expert_rows.T, grad_logits_half)
    grad_normed_rows = matmul(pick_any.T, grad_table) + matmul(grad_logits_half, full_router.T)
    grad_gain_two = jnp.sum(grad_normed_rows * normed_two, 0)
    grad_bias_two = jnp.sum(grad_normed_rows, 0)
    grad_residual = upstream + norm_backward(grad_normed_rows * gain_two, normed_two, inverse_two)

    all_grad_res = seq_gather(grad_residual.astype(bf16)).reshape(-1, D)
    grad_mixed = matmul(all_grad_res, w_out_rows.T).astype(bf16)
    grad_qkv = jnp.concatenate(
        attend_back(query_rows, key_rows, value_rows, head_mixed, logsum, grad_mixed), 1
    )
    grad_normed = matmul(grad_qkv, w_heads.T)
    grad_weights = jnp.concatenate(
        [matmul(all_normed_in.T, grad_qkv), matmul(all_grad_res.T, head_mixed)], 1
    )
    grad_weights = grad_weights.astype(bf16).reshape(fsdp_size, D // fsdp_size, 4 * head_cols)
    grad_weights = lax.all_to_all(grad_weights, "fsdp", split_axis=0, concat_axis=0, tiled=True)
    grad_weights = jnp.sum(grad_weights.astype(f32), 0)
    own_grad_normed = seq_reduce(grad_normed.astype(bf16).reshape(seq_size, token_count, D))
    grad_tokens = grad_residual + norm_backward(
        own_grad_normed * gain_one, all_normed[:token_count], all_inverse[:token_count]
    )
    small_sums = jnp.concatenate(
        [
            grad_router,
            jnp.sum(grad_normed * all_normed, 0)[:, None],
            jnp.sum(grad_normed, 0)[:, None],
            grad_gain_two[:, None],
            grad_bias_two[:, None],
        ],
        1,
    )
    small_sums = lax.all_to_all(
        small_sums.reshape(devices, shard, -1),
        ("fsdp", "seq"),
        split_axis=0,
        concat_axis=0,
        tiled=True,
    )
    small_sums = jnp.sum(small_sums, 0)
    return (
        block_out[None],
        grad_tokens[None],
        small_sums[:, EXPERTS],
        small_sums[:, EXPERTS + 1],
        grad_weights[:, :head_cols],
        grad_weights[:, head_cols : 2 * head_cols],
        grad_weights[:, 2 * head_cols : 3 * head_cols],
        grad_weights[:, 3 * head_cols :].T,
        small_sums[:, EXPERTS + 2],
        small_sums[:, EXPERTS + 3],
        small_sums[:, :EXPERTS],
        grad_expert_in,
        grad_expert_out,
    )


def solution(mesh):
    return jax.shard_map(
        body,
        mesh=mesh,
        in_specs=(
            P("fsdp", "seq", None),
            P("fsdp", "seq", None),
            P(("fsdp", "seq")),
            P(("fsdp", "seq")),
            P(("fsdp", "seq"), None),
            P(("fsdp", "seq"), None),
            P(("fsdp", "seq"), None),
            P(("fsdp", "seq"), None),
            P(("fsdp", "seq")),
            P(("fsdp", "seq")),
            P(("fsdp", "seq"), None),
            P("fsdp", None, "seq"),
            P("fsdp", "seq", None),
            P("fsdp", "seq", None),
        ),
        out_specs=(
            P("fsdp", "seq", None),
            P("fsdp", "seq", None),
            P(("fsdp", "seq")),
            P(("fsdp", "seq")),
            P("fsdp", "seq"),
            P("fsdp", "seq"),
            P("fsdp", "seq"),
            P("seq", "fsdp"),
            P(("fsdp", "seq")),
            P(("fsdp", "seq")),
            P(("fsdp", "seq"), None),
            P("fsdp", None, "seq"),
            P("fsdp", "seq", None),
        ),
        check_vma=False,
    )
```

```python
import functools

import jax
import jax.numpy as jnp
from jax import lax
from jax.experimental import pallas as pl
from jax.experimental.pallas import tpu as pltpu
from jax.sharding import PartitionSpec as P

D = 768
HEAD_DIM = 64
EXPERTS = 32
TOP = 2
CAP = 10


EPS = 1e-06
TANH_SCALE = 0.7978845608028654
CUBIC = 0.044715


def matmul(left_side, right_side):
    return jnp.dot(left_side, right_side, preferred_element_type=jnp.float32)


def matmul_t(left_side, right_side):
    return lax.dot_general(
        left_side, right_side, (((1,), (1,)), ((), ())), preferred_element_type=jnp.float32
    )


def t_matmul(left_side, right_side):
    return lax.dot_general(
        left_side, right_side, (((0,), (0,)), ((), ())), preferred_element_type=jnp.float32
    )


def norm_forward(values):
    centre = values - jnp.mean(values, -1, keepdims=True)
    inverse = lax.rsqrt(jnp.mean(centre * centre, -1, keepdims=True) + EPS)
    return (centre * inverse, inverse)


def norm_backward(grad_normed, normed, inverse):
    return inverse * (
        grad_normed
        - jnp.mean(grad_normed, -1, keepdims=True)
        - normed * jnp.mean(grad_normed * normed, -1, keepdims=True)
    )


def gelu_both(inner_act):
    square = inner_act * inner_act
    bent = jnp.tanh(TANH_SCALE * inner_act * (1.0 + CUBIC * square))
    value = 0.5 * inner_act * (1.0 + bent)
    slope = 0.5 * (1.0 + bent) + 0.5 * inner_act * (1.0 - bent * bent) * TANH_SCALE * (
        1.0 + 3.0 * CUBIC * square
    )
    return (value, slope)


SCALING = HEAD_DIM ** (-0.5)
MIB = 1024 * 1024
WHOLE = pl.BlockSpec(memory_space=pltpu.VMEM)


def call(kernel, outputs, operands, after=(), fresh=(), scratch=(), flops=0, mib=20):
    moved = sum(v.size * v.dtype.itemsize for v in operands)
    used = len(operands)

    def inner(*refs):
        kernel(*refs[:used], *refs[used + len(after) :])

    operands = [
        operand if index in fresh else in_hbm([operand])[0]
        for index, operand in enumerate(operands)
    ] + in_hbm(after)
    return pl.pallas_call(
        inner,
        out_shape=outputs,
        in_specs=[WHOLE] * used + [pl.BlockSpec(memory_space=pl.ANY)] * len(after),
        out_specs=[WHOLE] * len(outputs),
        scratch_shapes=scratch,
        cost_estimate=pl.CostEstimate(flops=flops, bytes_accessed=moved, transcendentals=0),
        compiler_params=pltpu.CompilerParams(vmem_limit_bytes=mib * MIB),
    )(*operands)


def shaped(dtype, *shape):
    return pltpu.HBM(shape, dtype)


def in_hbm(operands):
    return [pltpu.with_memory_space_constraint(operand, pltpu.HBM) for operand in operands]


def held_back(array, other):
    anywhere = pl.BlockSpec(memory_space=pl.ANY)
    return pl.pallas_call(
        lambda array_ref, other_ref, out_ref: None,
        out_shape=shaped(array.dtype, *array.shape),
        in_specs=[anywhere, anywhere],
        out_specs=anywhere,
        input_output_aliases={0: 0},
    )(*in_hbm([array]), other)


def attend_kernel(
    own, far, near, diag, held, normed_ref, normed_in_ref, qkv_ref, mixed_ref, logsum_ref, vec_ref
):
    bf16 = jnp.bfloat16
    f32 = jnp.float32
    columns = qkv_ref.shape[1]
    lanes = held.shape[1]
    wanted = lax.broadcasted_iota(jnp.int32, (8, lanes), 0) + (columns + EXPERTS)
    picker = (lax.broadcasted_iota(jnp.int32, (8, lanes), 1) == wanted).astype(bf16)
    vectors = matmul_t(picker, held[...])
    vec_ref[...] = vectors
    count = own.shape[0]
    for index, block in enumerate((own, far, near, diag)):
        normed, _ = norm_forward(block[...])
        rows = pl.ds(index * count, count)
        normed_ref[rows, :] = normed
        normed_in_ref[rows, :] = (normed * vectors[0:1] + vectors[1:2]).astype(bf16)
    qkv_ref[...] = matmul(normed_in_ref[...], held[:, :columns]).astype(bf16)
    width = columns // 3
    logsum_ref[...] = jnp.zeros_like(logsum_ref)
    for low in range(0, width, HEAD_DIM):
        query = qkv_ref[:, low : low + HEAD_DIM]
        key = qkv_ref[:, width + low : width + low + HEAD_DIM]
        value = qkv_ref[:, 2 * width + low : 2 * width + low + HEAD_DIM]
        scores = matmul_t(query, key) * SCALING
        highest = jnp.max(scores, -1, keepdims=True)
        raised = jnp.exp(scores - highest)
        total = jnp.sum(raised, -1, keepdims=True)
        head = low // HEAD_DIM
        logsum_ref[:, head : head + 1] = highest + jnp.log(total)
        weights = (raised * (1.0 / total)).astype(bf16)
        mixed_ref[:, low : low + HEAD_DIM] = matmul(weights, value).astype(bf16)


def attend_back_kernel(
    own,
    far,
    near,
    diag,
    w_out,
    held,
    qkv,
    mixed,
    logsum,
    normed,
    normed_in,
    small,
    gn_own,
    gn_far,
    gn_near,
    gn_diag,
    dw_ref,
    gr_ref,
    gqkv_ref,
):
    bf16 = jnp.bfloat16
    f32 = jnp.float32
    count = own.shape[0]
    columns = qkv.shape[1]
    width = columns // 3
    for index, block in enumerate((own, far, near, diag)):
        gr_ref[pl.ds(index * count, count), :] = block[...]
    grad_mixed = matmul_t(gr_ref[...], w_out[...]).astype(bf16)
    for low in range(0, width, HEAD_DIM):
        head = low // HEAD_DIM
        query = qkv[:, low : low + HEAD_DIM]
        key = qkv[:, width + low : width + low + HEAD_DIM]
        value = qkv[:, 2 * width + low : 2 * width + low + HEAD_DIM]
        grad_head = grad_mixed[:, low : low + HEAD_DIM]
        delta = jnp.sum(
            grad_head.astype(f32) * mixed[:, low : low + HEAD_DIM].astype(f32), -1, keepdims=True
        )
        probs = jnp.exp(matmul_t(query, key) * SCALING - logsum[:, head : head + 1])
        grad_probs = matmul_t(grad_head, value)
        grad_scores = (probs * (grad_probs - delta) * SCALING).astype(bf16)
        gqkv_ref[:, low : low + HEAD_DIM] = matmul(grad_scores, key).astype(bf16)
        gqkv_ref[:, width + low : width + low + HEAD_DIM] = t_matmul(grad_scores, query).astype(
            bf16
        )
        gqkv_ref[:, 2 * width + low : 2 * width + low + HEAD_DIM] = t_matmul(
            probs.astype(bf16), grad_head
        ).astype(bf16)
    grad_normed = matmul_t(gqkv_ref[...], held[:, :columns])
    for index, block in enumerate((gn_own, gn_far, gn_near, gn_diag)):
        block[...] = grad_normed[index * count : (index + 1) * count].astype(bf16)
    dw_ref[:, :columns] = t_matmul(normed_in[...], gqkv_ref[...]).astype(bf16)
    dw_ref[:, columns : columns + width] = t_matmul(gr_ref[...], mixed[...]).astype(bf16)
    gain_row = jnp.sum(grad_normed * normed[...], 0, keepdims=True)
    bias_row = jnp.sum(grad_normed, 0, keepdims=True)
    row = lax.broadcasted_iota(jnp.int32, (8, gain_row.shape[1]), 0)
    both = jnp.where(row == 0, gain_row, jnp.where(row == 1, bias_row, 0.0))
    sums = small[...] + columns_of(both, EXPERTS, small.shape[1])
    high = sums.astype(bf16)
    low = columns + width
    dw_ref[:, low:] = jnp.zeros((dw_ref.shape[0], dw_ref.shape[1] - low), bf16)
    dw_ref[:, low : low + sums.shape[1]] = high
    dw_ref[:, low + HEAD_DIM : low + HEAD_DIM + sums.shape[1]] = (
        sums - high.astype(f32)
    ).astype(bf16)


def columns_of(rows, first, lanes):
    count = rows.shape[0]
    spots = lax.broadcasted_iota(jnp.int32, (count, lanes), 1)
    placed = (spots == lax.broadcasted_iota(jnp.int32, (count, lanes), 0) + first).astype(
        jnp.float32
    )
    return lax.dot_general(
        rows,
        placed,
        (((0,), (0,)), ((), ())),
        preferred_element_type=jnp.float32,
        precision=lax.Precision.HIGHEST,
    )


def picks_of(position, choice, rows, copies):
    spots = lax.broadcasted_iota(jnp.int32, (position.shape[0], rows), 1)
    first = position[:, choice : choice + 1]
    hit = spots == first
    for copy in range(1, copies):
        hit = hit | (spots == first + copy * CAP)
    return hit.astype(jnp.float32)


def gates_of(probs, chosen, choice):
    spots = lax.broadcasted_iota(jnp.int32, probs.shape, 1)
    return jnp.sum(
        jnp.where(spots == chosen[:, choice : choice + 1], probs, 0.0), -1, keepdims=True
    )


def route_kernel(
    tokens_in, own, near, far, vectors, router, position, residual_ref, rows_ref, probs_ref, table_ref,
    *, copies
):
    bf16 = jnp.bfloat16
    f32 = jnp.float32
    residual = tokens_in[...] + (
        own[...].astype(f32) + near[...].astype(f32) + far[...].astype(f32)
    )
    residual_ref[...] = residual
    normed, _ = norm_forward(residual)
    rows = (normed * vectors[2:3, :] + vectors[3:4, :]).astype(bf16)
    rows_ref[...] = rows
    logits = matmul(rows, router[...])
    raised = jnp.exp(logits - jnp.max(logits, -1, keepdims=True))
    probs_ref[...] = raised / jnp.sum(raised, -1, keepdims=True)
    size = table_ref.shape[0]
    spots = picks_of(position[...], 0, size, copies) + picks_of(position[...], 1, size, copies)
    table_ref[...] = t_matmul(spots.astype(bf16), rows).astype(bf16)


def combine_kernel(
    residual, upstream, vectors, router, rows, probs, chosen, position, route_dots, table,
    own, near, far, regroup,
    grad_ref, half_ref, small_ref, settled_ref, *, copies
):
    bf16 = jnp.bfloat16
    f32 = jnp.float32
    size = table.shape[0]
    picks = [picks_of(position[...], choice, size, copies) for choice in range(TOP)]
    grad_probs = jnp.zeros(probs.shape, f32)
    spots = lax.broadcasted_iota(jnp.int32, probs.shape, 1)
    for choice in range(TOP):
        grad_gate = jnp.sum(picks[choice] * route_dots[0:1, :], -1, keepdims=True)
        grad_probs = grad_probs + jnp.where(
            spots == chosen[:, choice : choice + 1], grad_gate, 0.0
        )
    shares = probs[...]
    grad_logits = shares * (grad_probs - jnp.sum(shares * grad_probs, -1, keepdims=True))
    grad_logits = grad_logits.astype(bf16)
    grad_rows = matmul((picks[0] + picks[1]).astype(bf16), table[...]) + matmul_t(
        grad_logits, router[...]
    )
    normed, inverse = norm_forward(residual[...])
    grad = upstream[...] + norm_backward(grad_rows * vectors[2:3, :], normed, inverse)
    grad_ref[...] = grad
    half_ref[...] = grad.astype(bf16)
    gain_row = jnp.sum(grad_rows * normed, 0, keepdims=True)
    bias_row = jnp.sum(grad_rows, 0, keepdims=True)
    row = lax.broadcasted_iota(jnp.int32, (8, gain_row.shape[1]), 0)
    both = jnp.where(row == 0, gain_row, jnp.where(row == 1, bias_row, 0.0))
    lanes = small_ref.shape[1]
    small_ref[...] = columns_of(both, EXPERTS + 2, lanes)
    small_ref[:, :EXPERTS] = t_matmul(rows[...], grad_logits)
    settle_kernel(own, near, far, regroup, settled_ref)


def block_out_kernel(residual, probs, chosen, position, table, out_ref, *, copies):
    out = residual[...]
    for choice in range(TOP):
        pick = picks_of(position[...], choice, table.shape[0], copies).astype(jnp.bfloat16)
        out = out + gates_of(probs[...], chosen, choice) * matmul(pick, table[...])
    out_ref[...] = out


def expert_kernel(
    first,
    x_own, x_far, x_near, x_diag,
    c_own, c_far, c_near, c_diag,
    router, w_in, w_out,
    o_own, o_far, o_near, o_diag,
    g_own, g_far, g_near, g_diag,
    rows_ref, cots_ref, hidden_ref, inner_ref, dots_ref,
):
    bf16 = jnp.bfloat16
    f32 = jnp.float32
    count = x_own.shape[1]
    parts = [pl.ds(index * count, count) for index in range(4)]
    for part, block, cots in zip(
        parts, (x_own, x_far, x_near, x_diag), (c_own, c_far, c_near, c_diag)
    ):
        rows_ref[0, part, :] = block[0]
        cots_ref[0, part, :] = cots[0]
    rows = rows_ref[0]
    bare = cots_ref[0]
    logits = matmul(rows, router[...])
    raised = jnp.exp(logits - jnp.max(logits, -1, keepdims=True))
    wanted = first[0] + pl.program_id(0)
    spots = lax.broadcasted_iota(jnp.int32, logits.shape, 1)
    gate = jnp.sum(jnp.where(spots == wanted, raised, 0.0), -1, keepdims=True) / jnp.sum(
        raised, -1, keepdims=True
    )
    cots = (gate * bare.astype(f32)).astype(bf16)
    cots_ref[0] = cots
    out_sum = None
    for half in range(w_in.shape[0]):
        value, slope = gelu_both(matmul(rows, w_in[half]))
        hidden = value.astype(bf16)
        hidden_ref[half] = hidden
        inner = (matmul_t(cots, w_out[half]) * slope).astype(bf16)
        inner_ref[half] = inner
        out = matmul(hidden, w_out[half])
        grad = matmul_t(inner, w_in[half])
        out_sum = out if out_sum is None else out_sum + out
        grad_sum = grad if half == 0 else grad_sum + grad
    dots = jnp.sum(out_sum * bare.astype(f32), -1, keepdims=True)
    dots_ref[0] = jnp.broadcast_to(dots, dots_ref.shape[1:])
    for index, (out, grad) in enumerate(
        zip((o_own, o_far, o_near, o_diag), (g_own, g_far, g_near, g_diag))
    ):
        low = index * count
        out[0] = out_sum[low : low + count].astype(bf16)
        grad[0] = grad_sum[low : low + count].astype(bf16)


def experts(first, rows, cots, router, w_in, w_out):
    bf16 = jnp.bfloat16
    f32 = jnp.float32
    local_experts, count, _ = rows[0].shape
    slices, _, hidden_cols = w_in.shape
    halves = slices // local_experts
    total = 4 * count
    by_expert = pl.BlockSpec((1, count, D), lambda e: (e, 0, 0))
    by_expert_all = pl.BlockSpec((1, total, D), lambda e: (e, 0, 0))
    by_slice = lambda *shape: pl.BlockSpec((halves,) + shape, lambda e: (e, 0, 0))
    flops = 8 * slices * total * D * hidden_cols
    moved = 4 * slices * D * hidden_cols + 12 * local_experts * total * D
    return pl.pallas_call(
        expert_kernel,
        grid=(local_experts,),
        in_specs=[pl.BlockSpec(memory_space=pltpu.SMEM)]
        + [by_expert] * 8
        + [
            pl.BlockSpec((D, EXPERTS), lambda e: (0, 0)),
            by_slice(D, hidden_cols),
            by_slice(hidden_cols, D),
        ],
        out_specs=[by_expert] * 8
        + [
            by_expert_all,
            by_expert_all,
            by_slice(total, hidden_cols),
            by_slice(total, hidden_cols),
            pl.BlockSpec((1, total, 8), lambda e: (e, 0, 0)),
        ],
        out_shape=[shaped(bf16, local_experts, count, D)] * 8
        + [shaped(bf16, local_experts, total, D)] * 2
        + [shaped(bf16, slices, total, hidden_cols)] * 2
        + [shaped(f32, local_experts, total, 8)],
        cost_estimate=pl.CostEstimate(flops=flops, bytes_accessed=moved, transcendentals=0),
        compiler_params=pltpu.CompilerParams(
            vmem_limit_bytes=(28 if count <= 128 else 58) * MIB
        ),
    )(first, *rows, *cots, router, *in_hbm([w_in, w_out]))


def product_kernel(left, right, out_ref):
    for index in range(out_ref.shape[0]):
        out_ref[index] = t_matmul(
            left[min(index, left.shape[0] - 1)], right[min(index, right.shape[0] - 1)]
        )


def expert_products(left, right):
    slices = max(left.shape[0], right.shape[0])
    local_experts = min(left.shape[0], right.shape[0])
    shape = (left.shape[2], right.shape[2])
    block = lambda first, *rest: pl.BlockSpec((first // local_experts,) + rest, lambda e: (e, 0, 0))
    flops = 2 * slices * left.shape[1] * shape[0] * shape[1]
    return pl.pallas_call(
        product_kernel,
        grid=(local_experts,),
        in_specs=[block(*left.shape), block(*right.shape)],
        out_specs=block(slices, *shape),
        out_shape=shaped(jnp.float32, slices, *shape),
        cost_estimate=pl.CostEstimate(
            flops=flops,
            bytes_accessed=4 * slices * shape[0] * shape[1] + 2 * (left.size + right.size),
            transcendentals=0,
        ),
        compiler_params=pltpu.CompilerParams(
            vmem_limit_bytes=(16 if left.shape[1] <= 512 else 48) * MIB
        ),
    )(*in_hbm([left, right]))


def settle_kernel(own, near, far, regroup, out_ref):
    f32 = jnp.float32
    summed = own[...].astype(f32) + near[...].astype(f32) + far[...].astype(f32)
    out_ref[...] = t_matmul(regroup[...], summed.astype(jnp.bfloat16)).astype(jnp.bfloat16)


def finish_kernel(received, query_ref, key_ref, value_ref, output_ref, small_ref):
    f32 = jnp.float32
    width = query_ref.shape[1]
    total = received[0].astype(f32)
    for index in range(1, received.shape[0]):
        total = total + received[index].astype(f32)
    query_ref[...] = total[:, :width]
    key_ref[...] = total[:, width : 2 * width]
    value_ref[...] = total[:, 2 * width : 3 * width]
    output_ref[...] = total[:, 3 * width : 4 * width].T
    low = 4 * width
    lanes = small_ref.shape[1]
    small_ref[...] = (
        total[:, low : low + lanes] + total[:, low + HEAD_DIM : low + HEAD_DIM + lanes]
    )


def weight_blocks_kernel(query, key, value, router, gain1, bias1, gain2, bias2, out_ref):
    bf16 = jnp.bfloat16
    devices_on, seq_size, shard, lanes = out_ref.shape
    width = query.shape[1] // seq_size
    spots = lax.broadcasted_iota(jnp.int32, (8, shard), 0)
    vectors = jnp.zeros((8, shard), bf16)
    for index, vector in enumerate((gain1, bias1, gain2, bias2)):
        vectors = jnp.where(spots == index, vector[...], vectors)
    tail = lanes - 3 * width
    where_to = lax.broadcasted_iota(jnp.int32, (8, tail), 0) + EXPERTS
    placed = (lax.broadcasted_iota(jnp.int32, (8, tail), 1) == where_to).astype(bf16)
    rest = t_matmul(vectors, placed).astype(bf16)
    for part in range(seq_size):
        low = part * width
        for index, matrix in enumerate((query, key, value)):
            block = matrix[:, low : low + width]
            for copy in range(devices_on):
                out_ref[copy, part, :, index * width : (index + 1) * width] = block
        for copy in range(devices_on):
            out_ref[copy, part, :, 3 * width :] = rest
            out_ref[copy, part, :, 3 * width : 3 * width + EXPERTS] = router[...]


FAR = [(index, index ^ 2) for index in range(4)]
NEAR = [(index, index ^ 1) for index in range(4)]


def seq_gather(block):
    far = lax.ppermute(block, "seq", FAR)
    return (block, far, lax.ppermute(block, "seq", NEAR), lax.ppermute(far, "seq", NEAR))


def seq_reduce(own, far, near, diag):
    beside = lax.ppermute(diag, "seq", NEAR)
    pair = (far.astype(jnp.float32) + beside.astype(jnp.float32)).astype(far.dtype)
    return (own, lax.ppermute(near, "seq", NEAR), lax.ppermute(pair, "seq", FAR))


def body(
    block_in,
    expert_ids,
    ln1_gain,
    ln1_bias,
    w_query,
    w_key,
    w_value,
    w_output,
    ln2_gain,
    ln2_bias,
    w_router,
    w_expert_in,
    w_expert_out,
    cotangent,
):
    bf16 = jnp.bfloat16
    f32 = jnp.float32
    fsdp_size = lax.axis_size("fsdp")
    seq_size = lax.axis_size("seq")
    devices = fsdp_size * seq_size
    shard = w_query.shape[0]
    head_cols = D // seq_size
    local_slices = w_expert_in.shape[0]
    local_experts = max(1, local_slices // 2)
    halves = local_slices // local_experts
    copies = 2 // halves
    tokens_in = block_in[0]
    upstream = cotangent[0]
    chosen = expert_ids[0]
    token_count = chosen.shape[0]

    moves = [
        (fsdp_size * part + place, seq_size * place + part)
        for part in range(seq_size)
        for place in range(fsdp_size)
    ]
    w_out_rows = lax.ppermute(w_output, ("fsdp", "seq"), moves)
    w_out_rows = jnp.broadcast_to(w_out_rows, (fsdp_size, shard, D))
    w_out_rows = lax.all_to_all(w_out_rows, "fsdp", split_axis=0, concat_axis=0, tiled=True)
    w_out_rows = w_out_rows.reshape(head_cols, D)
    sent = call(
        weight_blocks_kernel,
        [shaped(bf16, fsdp_size, seq_size, shard, 3 * head_cols + EXPERTS + 4)],
        [w_query, w_key, w_value, w_router]
        + [v.reshape(1, shard) for v in (ln1_gain, ln1_bias, ln2_gain, ln2_bias)],
    )[0].reshape(devices, shard, -1)
    held = lax.all_to_all(sent, ("fsdp", "seq"), split_axis=0, concat_axis=0, tiled=True)
    held = held.reshape(D, -1)

    hot = (chosen.reshape(-1)[:, None] == jnp.arange(EXPERTS)[None, :]).astype(bf16)
    routes = token_count * TOP
    earlier = (jnp.arange(routes)[:, None] > jnp.arange(routes)[None, :]).astype(bf16)
    slot = jnp.sum(matmul(earlier, hot) * hot.astype(f32), 1).astype(jnp.int32)
    position = chosen * (CAP * copies) + slot.reshape(token_count, TOP)
    table_rows = EXPERTS * copies * CAP
    local_rows = local_experts * fsdp_size * CAP
    spot = jnp.arange(local_rows)
    source_of = (spot // CAP % fsdp_size) * (local_experts * CAP) + (
        spot // (CAP * fsdp_size) * CAP + spot % CAP
    )
    regroup = (source_of[:, None] == spot[None, :]).astype(bf16)

    def to_experts(table):
        table = table.reshape(fsdp_size, local_experts * CAP, D)
        received = lax.all_to_all(table, "fsdp", split_axis=0, concat_axis=0, tiled=True)
        grouped = matmul(regroup, received.reshape(local_rows, D)).astype(bf16)
        return seq_gather(grouped.reshape(local_experts, fsdp_size * CAP, D))

    def settle(partial, after):
        blocks = [part.reshape(local_rows, D) for part in seq_reduce(*partial)]
        return call(
            settle_kernel,
            [shaped(bf16, local_rows, D)],
            [*blocks, regroup],
            after=after,
            fresh=(1, 2),
            flops=2 * local_rows * local_rows * D,
        )[0]

    def from_experts(settled):
        returned = lax.all_to_all(
            settled.reshape(fsdp_size, local_experts * CAP, D),
            "fsdp",
            split_axis=0,
            concat_axis=0,
            tiled=True,
        )
        return returned.reshape(table_rows, D)

    image = token_count * seq_size
    columns = 3 * head_cols
    router = held[:, columns : columns + EXPERTS]
    normed_one, normed_in, qkv, head_mixed, logsum, vectors = call(
        attend_kernel,
        [
            shaped(f32, image, D),
            shaped(bf16, image, D),
            shaped(bf16, image, columns),
            shaped(bf16, image, head_cols),
            shaped(f32, image, 8),
            shaped(f32, 8, D),
        ],
        [*seq_gather(tokens_in), held],
        fresh=(1, 2, 3, 4),
        flops=2 * image * D * columns + 4 * image * image * head_cols,
    )
    out_partial = matmul(head_mixed, w_out_rows).astype(bf16)
    out_blocks = [out_partial[i * token_count : (i + 1) * token_count] for i in range(seq_size)]

    residual, expert_rows, router_probs, rows_table = call(
        functools.partial(route_kernel, copies=copies),
        [
            shaped(f32, token_count, D),
            shaped(bf16, token_count, D),
            shaped(f32, token_count, EXPERTS),
            shaped(bf16, table_rows, D),
        ],
        [tokens_in, *seq_reduce(*out_blocks), vectors, router, position],
        fresh=(1, 2, 3, 6),
    )
    spots = jnp.arange(table_rows)[None, None, :] - position[:, :, None]
    hits = (spots == 0) if copies == 1 else ((spots == 0) | (spots == CAP))
    cots_table = t_matmul(jnp.any(hits, 1).astype(bf16), upstream.astype(bf16)).astype(bf16)
    slot_cots = to_experts(cots_table)
    slot_rows = to_experts(rows_table)

    first = (lax.axis_index("fsdp") * local_slices // 2).astype(jnp.int32).reshape(1)
    results = experts(
        first,
        slot_rows,
        slot_cots,
        router,
        w_expert_in,
        w_expert_out,
    )
    out_parts, grad_parts = results[:4], results[4:8]
    all_rows, all_cots, hidden_act, grad_inner, dots = results[8:]
    grad_expert_in = expert_products(all_rows, grad_inner)
    grad_expert_out = expert_products(hidden_act, all_cots)
    me = lax.axis_index("seq")
    turned = jnp.array([0, 2, 1, 3])[me ^ jnp.arange(seq_size)]
    dots = dots[:, :, 0].reshape(local_experts, seq_size, fsdp_size, CAP)
    dots = jnp.take(dots.transpose(2, 1, 0, 3), turned, axis=1)
    dots = lax.all_to_all(
        dots.reshape(devices, 1, local_experts * CAP),
        ("fsdp", "seq"),
        split_axis=0,
        concat_axis=0,
        tiled=True,
    )
    route_dots = jnp.sum(dots.reshape(fsdp_size, seq_size, -1), 1).reshape(1, table_rows)
    grad_table = from_experts(settle(grad_parts, [grad_expert_in]))
    grad_residual, grad_res_half, small_sums, out_settled = call(
        functools.partial(combine_kernel, copies=copies),
        [
            shaped(f32, token_count, D),
            shaped(bf16, token_count, D),
            shaped(f32, D, EXPERTS + 4),
            shaped(bf16, local_rows, D),
        ],
        [
            residual,
            upstream,
            vectors,
            router,
            expert_rows,
            router_probs,
            chosen,
            position,
            route_dots,
            grad_table,
            *[block.reshape(local_rows, D) for block in seq_reduce(*out_parts)],
            regroup,
        ],
        after=[grad_expert_out],
        fresh=(6, 7, 8, 9, 11, 12),
    )

    out_table = from_experts(out_settled)
    block_out = call(
        functools.partial(block_out_kernel, copies=copies),
        [shaped(f32, token_count, D)],
        [residual, router_probs, chosen, position, out_table],
        fresh=(2, 3, 4),
    )[0]

    *gn_parts, grad_weights = call(
        attend_back_kernel,
        [shaped(bf16, token_count, D)] * 4
        + [shaped(bf16, D, 4 * head_cols + 2 * HEAD_DIM)],
        [
            *seq_gather(grad_res_half),
            w_out_rows,
            held,
            qkv,
            head_mixed,
            logsum,
            normed_one,
            normed_in,
            small_sums,
        ],
        fresh=(1, 2, 3, 4),
        scratch=[pltpu.VMEM((image, D), bf16), pltpu.VMEM((image, columns), bf16)],
        flops=4 * (4 * image * D * 4 * head_cols + 10 * image * image * head_cols),
    )
    grad_weights = held_back(grad_weights, out_table)
    grad_weights = lax.all_to_all(
        grad_weights.reshape(fsdp_size, D // fsdp_size, 4 * head_cols + 2 * HEAD_DIM),
        "fsdp",
        split_axis=0,
        concat_axis=0,
        tiled=True,
    )
    *grad_squares, small_sums = call(
        finish_kernel,
        [shaped(f32, D // fsdp_size, head_cols)] * 3
        + [shaped(f32, head_cols, D // fsdp_size), shaped(f32, D // fsdp_size, EXPERTS + 4)],
        [grad_weights],
        after=[block_out],
        fresh=(0,),
    )
    place = lax.axis_index("seq")
    for step, swap in ((2, FAR), (1, NEAR)):
        rows = small_sums.shape[0] // 2
        upper = (place // step) % 2
        away = lax.dynamic_slice_in_dim(small_sums, (1 - upper) * rows, rows)
        kept = lax.dynamic_slice_in_dim(small_sums, upper * rows, rows)
        small_sums = kept + lax.ppermute(away, "seq", swap)
    own, near, far = seq_reduce(*gn_parts)
    own_grad_normed = own.astype(f32) + near.astype(f32) + far.astype(f32)
    own_normed, own_inverse = norm_forward(tokens_in)
    grad_tokens = grad_residual + norm_backward(
        own_grad_normed * vectors[0], own_normed, own_inverse
    )
    return (
        block_out[None],
        grad_tokens[None],
        small_sums[:, EXPERTS],
        small_sums[:, EXPERTS + 1],
        *grad_squares,
        small_sums[:, EXPERTS + 2],
        small_sums[:, EXPERTS + 3],
        small_sums[:, :EXPERTS],
        grad_expert_in,
        grad_expert_out,
    )


def solution(mesh):
    return jax.shard_map(
        body,
        mesh=mesh,
        in_specs=(
            P("fsdp", "seq", None),
            P("fsdp", "seq", None),
            P(("fsdp", "seq")),
            P(("fsdp", "seq")),
            P(("fsdp", "seq"), None),
            P(("fsdp", "seq"), None),
            P(("fsdp", "seq"), None),
            P(("fsdp", "seq"), None),
            P(("fsdp", "seq")),
            P(("fsdp", "seq")),
            P(("fsdp", "seq"), None),
            P("fsdp", None, "seq"),
            P("fsdp", "seq", None),
            P("fsdp", "seq", None),
        ),
        out_specs=(
            P("fsdp", "seq", None),
            P("fsdp", "seq", None),
            P(("fsdp", "seq")),
            P(("fsdp", "seq")),
            P("fsdp", "seq"),
            P("fsdp", "seq"),
            P("fsdp", "seq"),
            P("seq", "fsdp"),
            P(("fsdp", "seq")),
            P(("fsdp", "seq")),
            P(("fsdp", "seq"), None),
            P("fsdp", None, "seq"),
            P("fsdp", "seq", None),
        ),
        check_vma=False,
    )
```

```python
import functools

import jax
import jax.numpy as jnp
from jax import lax
from jax.experimental import pallas as pl
from jax.experimental.pallas import tpu as pltpu
from jax.sharding import PartitionSpec as P

D = 768
HEAD_DIM = 64
EXPERTS = 32
TOP = 2
CAP = 10


EPS = 1e-06
TANH_SCALE = 0.7978845608028654
CUBIC = 0.044715


def matmul(left_side, right_side):
    return jnp.dot(left_side, right_side, preferred_element_type=jnp.float32)


def matmul_t(left_side, right_side):
    return lax.dot_general(
        left_side, right_side, (((1,), (1,)), ((), ())), preferred_element_type=jnp.float32
    )


def t_matmul(left_side, right_side):
    return lax.dot_general(
        left_side, right_side, (((0,), (0,)), ((), ())), preferred_element_type=jnp.float32
    )


def norm_forward(values):
    centre = values - jnp.mean(values, -1, keepdims=True)
    inverse = lax.rsqrt(jnp.mean(centre * centre, -1, keepdims=True) + EPS)
    return (centre * inverse, inverse)


def norm_backward(grad_normed, normed, inverse):
    return inverse * (
        grad_normed
        - jnp.mean(grad_normed, -1, keepdims=True)
        - normed * jnp.mean(grad_normed * normed, -1, keepdims=True)
    )


def gelu_both(inner_act):
    square = inner_act * inner_act
    bent = jnp.tanh(TANH_SCALE * inner_act * (1.0 + CUBIC * square))
    value = 0.5 * inner_act * (1.0 + bent)
    slope = 0.5 * (1.0 + bent) + 0.5 * inner_act * (1.0 - bent * bent) * TANH_SCALE * (
        1.0 + 3.0 * CUBIC * square
    )
    return (value, slope)


SCALING = HEAD_DIM ** (-0.5)
MIB = 1024 * 1024
WHOLE = pl.BlockSpec(memory_space=pltpu.VMEM)


def call(kernel, outputs, operands, after=(), fresh=(), scalars=(), scratch=(), flops=0, mib=20, light=False):
    moved = 0 if light else sum(v.size * v.dtype.itemsize for v in operands)
    used = len(operands)

    def inner(*refs):
        kernel(*refs[:used], *refs[used + len(after) :])

    operands = [
        operand if index in fresh or index in scalars else in_hbm([operand])[0]
        for index, operand in enumerate(operands)
    ] + in_hbm(after)
    return pl.pallas_call(
        inner,
        out_shape=outputs,
        in_specs=[
            pl.BlockSpec(memory_space=pltpu.SMEM) if index in scalars else WHOLE
            for index in range(used)
        ]
        + [pl.BlockSpec(memory_space=pl.ANY)] * len(after),
        out_specs=[WHOLE] * len(outputs),
        scratch_shapes=scratch,
        cost_estimate=pl.CostEstimate(flops=flops, bytes_accessed=moved, transcendentals=0),
        compiler_params=pltpu.CompilerParams(vmem_limit_bytes=mib * MIB),
    )(*operands)


def shaped(dtype, *shape):
    return pltpu.HBM(shape, dtype)


def in_hbm(operands):
    return [pltpu.with_memory_space_constraint(operand, pltpu.HBM) for operand in operands]


def held_back(array, other):
    anywhere = pl.BlockSpec(memory_space=pl.ANY)
    return pl.pallas_call(
        lambda array_ref, other_ref, out_ref: None,
        out_shape=shaped(array.dtype, *array.shape),
        in_specs=[anywhere, anywhere],
        out_specs=anywhere,
        input_output_aliases={0: 0},
    )(*in_hbm([array]), other)


def first_norm_kernel(tokens, normed_ref):
    normed_ref[...] = norm_forward(tokens[...])[0].astype(jnp.bfloat16)


def attend_kernel(
    own, far, near, diag, held_own, held_other, parity,
    normed_ref, normed_in_ref, qkv_ref, mixed_ref, logsum_ref, vec_ref, held_ref
):
    bf16 = jnp.bfloat16
    f32 = jnp.float32
    columns = qkv_ref.shape[1]
    outer, _, rows, lanes = held_ref.shape
    bit = parity[0]
    for place in range(outer):
        held_ref[place, bit] = held_own[place]
        held_ref[place, 1 - bit] = held_other[place]
    held = held_ref[...].reshape(outer * 2 * rows, lanes)
    wanted = lax.broadcasted_iota(jnp.int32, (8, lanes), 0) + (columns + EXPERTS)
    picker = (lax.broadcasted_iota(jnp.int32, (8, lanes), 1) == wanted).astype(bf16)
    vectors = matmul_t(picker, held)
    vec_ref[...] = vectors
    count = own.shape[0]
    for index, block in enumerate((own, far, near, diag)):
        normed = block[...].astype(f32)
        rows = pl.ds(index * count, count)
        normed_ref[rows, :] = block[...]
        normed_in_ref[rows, :] = (normed * vectors[0:1] + vectors[1:2]).astype(bf16)
    qkv_ref[...] = matmul(normed_in_ref[...], held[:, :columns]).astype(bf16)
    width = columns // 3
    logsum_ref[...] = jnp.zeros_like(logsum_ref)
    for low in range(0, width, HEAD_DIM):
        query = qkv_ref[:, low : low + HEAD_DIM]
        key = qkv_ref[:, width + low : width + low + HEAD_DIM]
        value = qkv_ref[:, 2 * width + low : 2 * width + low + HEAD_DIM]
        scores = matmul_t(query, key) * SCALING
        highest = jnp.max(scores, -1, keepdims=True)
        raised = jnp.exp(scores - highest)
        total = jnp.sum(raised, -1, keepdims=True)
        head = low // HEAD_DIM
        logsum_ref[:, head : head + 1] = highest + jnp.log(total)
        weights = (raised * (1.0 / total)).astype(bf16)
        mixed_ref[:, low : low + HEAD_DIM] = matmul(weights, value).astype(bf16)


def attend_back_kernel(
    own,
    far,
    near,
    diag,
    w_out,
    held,
    qkv,
    mixed,
    logsum,
    normed,
    normed_in,
    small,
    gn_own,
    gn_far,
    gn_near,
    gn_diag,
    dw_ref,
    gr_ref,
    gqkv_ref,
):
    bf16 = jnp.bfloat16
    f32 = jnp.float32
    count = own.shape[0]
    columns = qkv.shape[1]
    width = columns // 3
    for index, block in enumerate((own, far, near, diag)):
        gr_ref[pl.ds(index * count, count), :] = block[...]
    grad_mixed = matmul_t(gr_ref[...], w_out[...]).astype(bf16)
    for low in range(0, width, HEAD_DIM):
        head = low // HEAD_DIM
        query = qkv[:, low : low + HEAD_DIM]
        key = qkv[:, width + low : width + low + HEAD_DIM]
        value = qkv[:, 2 * width + low : 2 * width + low + HEAD_DIM]
        grad_head = grad_mixed[:, low : low + HEAD_DIM]
        delta = jnp.sum(
            grad_head.astype(f32) * mixed[:, low : low + HEAD_DIM].astype(f32), -1, keepdims=True
        )
        probs = jnp.exp(matmul_t(query, key) * SCALING - logsum[:, head : head + 1])
        grad_probs = matmul_t(grad_head, value)
        grad_scores = (probs * (grad_probs - delta) * SCALING).astype(bf16)
        gqkv_ref[:, low : low + HEAD_DIM] = matmul(grad_scores, key).astype(bf16)
        gqkv_ref[:, width + low : width + low + HEAD_DIM] = t_matmul(grad_scores, query).astype(
            bf16
        )
        gqkv_ref[:, 2 * width + low : 2 * width + low + HEAD_DIM] = t_matmul(
            probs.astype(bf16), grad_head
        ).astype(bf16)
    grad_normed = matmul_t(gqkv_ref[...], held[:, :columns])
    for index, block in enumerate((gn_own, gn_far, gn_near, gn_diag)):
        block[...] = grad_normed[index * count : (index + 1) * count].astype(bf16)
    dw_ref[:, :columns] = t_matmul(normed_in[...], gqkv_ref[...]).astype(bf16)
    dw_ref[:, columns : columns + width] = t_matmul(gr_ref[...], mixed[...]).astype(bf16)
    gain_row = jnp.sum(grad_normed * normed[...].astype(f32), 0, keepdims=True)
    bias_row = jnp.sum(grad_normed, 0, keepdims=True)
    row = lax.broadcasted_iota(jnp.int32, (8, gain_row.shape[1]), 0)
    both = jnp.where(row == 0, gain_row, jnp.where(row == 1, bias_row, 0.0))
    sums = small[...] + columns_of(both, EXPERTS, small.shape[1])
    high = sums.astype(bf16)
    low = columns + width
    dw_ref[:, low:] = jnp.zeros((dw_ref.shape[0], dw_ref.shape[1] - low), bf16)
    dw_ref[:, low : low + sums.shape[1]] = high
    dw_ref[:, low + HEAD_DIM : low + HEAD_DIM + sums.shape[1]] = (
        sums - high.astype(f32)
    ).astype(bf16)


def columns_of(rows, first, lanes):
    count = rows.shape[0]
    spots = lax.broadcasted_iota(jnp.int32, (count, lanes), 1)
    placed = (spots == lax.broadcasted_iota(jnp.int32, (count, lanes), 0) + first).astype(
        jnp.float32
    )
    return lax.dot_general(
        rows,
        placed,
        (((0,), (0,)), ((), ())),
        preferred_element_type=jnp.float32,
        precision=lax.Precision.HIGHEST,
    )


def picks_of(position, choice, rows, copies):
    spots = lax.broadcasted_iota(jnp.int32, (position.shape[0], rows), 1)
    first = position[:, choice : choice + 1]
    hit = spots == first
    for copy in range(1, copies):
        hit = hit | (spots == first + copy * CAP)
    return hit.astype(jnp.float32)


def gates_of(probs, chosen, choice):
    spots = lax.broadcasted_iota(jnp.int32, probs.shape, 1)
    return jnp.sum(
        jnp.where(spots == chosen[:, choice : choice + 1], probs, 0.0), -1, keepdims=True
    )


def route_kernel(
    tokens_in, own, near, far, vectors, router, position, residual_ref, rows_ref, probs_ref, table_ref,
    *, copies
):
    bf16 = jnp.bfloat16
    f32 = jnp.float32
    residual = tokens_in[...] + (
        own[...].astype(f32) + near[...].astype(f32) + far[...].astype(f32)
    )
    residual_ref[...] = residual
    normed, _ = norm_forward(residual)
    rows = (normed * vectors[2:3, :] + vectors[3:4, :]).astype(bf16)
    rows_ref[...] = rows
    logits = matmul(rows, router[...])
    raised = jnp.exp(logits - jnp.max(logits, -1, keepdims=True))
    probs_ref[...] = raised / jnp.sum(raised, -1, keepdims=True)
    size = table_ref.shape[0]
    spots = picks_of(position[...], 0, size, copies) + picks_of(position[...], 1, size, copies)
    table_ref[...] = t_matmul(spots.astype(bf16), rows).astype(bf16)


def combine_kernel(
    residual, upstream, vectors, router, rows, probs, chosen, position, route_dots, table,
    own, near, far, regroup,
    grad_ref, half_ref, small_ref, settled_ref, *, copies
):
    bf16 = jnp.bfloat16
    f32 = jnp.float32
    size = table.shape[0]
    picks = [picks_of(position[...], choice, size, copies) for choice in range(TOP)]
    grad_probs = jnp.zeros(probs.shape, f32)
    spots = lax.broadcasted_iota(jnp.int32, probs.shape, 1)
    for choice in range(TOP):
        grad_gate = jnp.sum(picks[choice] * route_dots[0:1, :], -1, keepdims=True)
        grad_probs = grad_probs + jnp.where(
            spots == chosen[:, choice : choice + 1], grad_gate, 0.0
        )
    shares = probs[...]
    grad_logits = shares * (grad_probs - jnp.sum(shares * grad_probs, -1, keepdims=True))
    grad_logits = grad_logits.astype(bf16)
    grad_rows = matmul((picks[0] + picks[1]).astype(bf16), table[...]) + matmul_t(
        grad_logits, router[...]
    )
    normed, inverse = norm_forward(residual[...])
    grad = upstream[...] + norm_backward(grad_rows * vectors[2:3, :], normed, inverse)
    grad_ref[...] = grad
    half_ref[...] = grad.astype(bf16)
    gain_row = jnp.sum(grad_rows * normed, 0, keepdims=True)
    bias_row = jnp.sum(grad_rows, 0, keepdims=True)
    row = lax.broadcasted_iota(jnp.int32, (8, gain_row.shape[1]), 0)
    both = jnp.where(row == 0, gain_row, jnp.where(row == 1, bias_row, 0.0))
    lanes = small_ref.shape[1]
    small_ref[...] = columns_of(both, EXPERTS + 2, lanes)
    small_ref[:, :EXPERTS] = t_matmul(rows[...], grad_logits)
    settle_kernel(own, near, far, regroup, settled_ref)


def block_out_kernel(residual, probs, chosen, position, table, out_ref, *, copies):
    out = residual[...]
    for choice in range(TOP):
        pick = picks_of(position[...], choice, table.shape[0], copies).astype(jnp.bfloat16)
        out = out + gates_of(probs[...], chosen, choice) * matmul(pick, table[...])
    out_ref[...] = out


def expert_kernel(
    first,
    x_own, x_far, x_near, x_diag,
    c_own, c_far, c_near, c_diag,
    router, w_in, w_out,
    o_own, o_far, o_near, o_diag,
    g_own, g_far, g_near, g_diag,
    rows_ref, cots_ref, hidden_ref, inner_ref, dots_ref,
):
    bf16 = jnp.bfloat16
    f32 = jnp.float32
    count = x_own.shape[1]
    parts = [pl.ds(index * count, count) for index in range(4)]
    for part, block, cots in zip(
        parts, (x_own, x_far, x_near, x_diag), (c_own, c_far, c_near, c_diag)
    ):
        rows_ref[0, part, :] = block[0]
        cots_ref[0, part, :] = cots[0]
    rows = rows_ref[0]
    bare = cots_ref[0]
    logits = matmul(rows, router[...])
    raised = jnp.exp(logits - jnp.max(logits, -1, keepdims=True))
    wanted = first[0] + pl.program_id(0)
    spots = lax.broadcasted_iota(jnp.int32, logits.shape, 1)
    gate = jnp.sum(jnp.where(spots == wanted, raised, 0.0), -1, keepdims=True) / jnp.sum(
        raised, -1, keepdims=True
    )
    cots = (gate * bare.astype(f32)).astype(bf16)
    cots_ref[0] = cots
    out_sum = None
    for half in range(w_in.shape[0]):
        value, slope = gelu_both(matmul(rows, w_in[half]))
        hidden = value.astype(bf16)
        hidden_ref[half] = hidden
        inner = (matmul_t(cots, w_out[half]) * slope).astype(bf16)
        inner_ref[half] = inner
        out = matmul(hidden, w_out[half])
        grad = matmul_t(inner, w_in[half])
        out_sum = out if out_sum is None else out_sum + out
        grad_sum = grad if half == 0 else grad_sum + grad
    dots = jnp.sum(out_sum * bare.astype(f32), -1, keepdims=True)
    dots_ref[0] = jnp.broadcast_to(dots, dots_ref.shape[1:])
    for index, (out, grad) in enumerate(
        zip((o_own, o_far, o_near, o_diag), (g_own, g_far, g_near, g_diag))
    ):
        low = index * count
        out[0] = out_sum[low : low + count].astype(bf16)
        grad[0] = grad_sum[low : low + count].astype(bf16)


def experts(first, rows, cots, router, w_in, w_out):
    bf16 = jnp.bfloat16
    f32 = jnp.float32
    local_experts, count, _ = rows[0].shape
    slices, _, hidden_cols = w_in.shape
    halves = slices // local_experts
    total = 4 * count
    by_expert = pl.BlockSpec((1, count, D), lambda e: (e, 0, 0))
    by_expert_all = pl.BlockSpec((1, total, D), lambda e: (e, 0, 0))
    by_slice = lambda *shape: pl.BlockSpec((halves,) + shape, lambda e: (e, 0, 0))
    flops = 8 * slices * total * D * hidden_cols
    moved = 4 * slices * D * hidden_cols + 12 * local_experts * total * D
    return pl.pallas_call(
        expert_kernel,
        grid=(local_experts,),
        in_specs=[pl.BlockSpec(memory_space=pltpu.SMEM)]
        + [by_expert] * 8
        + [
            pl.BlockSpec((D, EXPERTS), lambda e: (0, 0)),
            by_slice(D, hidden_cols),
            by_slice(hidden_cols, D),
        ],
        out_specs=[by_expert] * 8
        + [
            by_expert_all,
            by_expert_all,
            by_slice(total, hidden_cols),
            by_slice(total, hidden_cols),
            pl.BlockSpec((1, total, 8), lambda e: (e, 0, 0)),
        ],
        out_shape=[shaped(bf16, local_experts, count, D)] * 8
        + [shaped(bf16, local_experts, total, D)] * 2
        + [shaped(bf16, slices, total, hidden_cols)] * 2
        + [shaped(f32, local_experts, total, 8)],
        cost_estimate=pl.CostEstimate(flops=flops, bytes_accessed=moved, transcendentals=0),
        compiler_params=pltpu.CompilerParams(
            vmem_limit_bytes=(28 if count <= 128 else 58) * MIB
        ),
    )(first, *rows, *cots, router, *in_hbm([w_in, w_out]))


def product_kernel(left, right, out_ref):
    for index in range(out_ref.shape[0]):
        out_ref[index] = t_matmul(
            left[min(index, left.shape[0] - 1)], right[min(index, right.shape[0] - 1)]
        )


def expert_products(left, right):
    slices = max(left.shape[0], right.shape[0])
    local_experts = min(left.shape[0], right.shape[0])
    shape = (left.shape[2], right.shape[2])
    block = lambda first, *rest: pl.BlockSpec((first // local_experts,) + rest, lambda e: (e, 0, 0))
    flops = 2 * slices * left.shape[1] * shape[0] * shape[1]
    return pl.pallas_call(
        product_kernel,
        grid=(local_experts,),
        in_specs=[block(*left.shape), block(*right.shape)],
        out_specs=block(slices, *shape),
        out_shape=shaped(jnp.float32, slices, *shape),
        cost_estimate=pl.CostEstimate(
            flops=flops,
            bytes_accessed=4 * slices * shape[0] * shape[1] + 2 * (left.size + right.size),
            transcendentals=0,
        ),
        compiler_params=pltpu.CompilerParams(
            vmem_limit_bytes=(16 if left.shape[1] <= 512 else 48) * MIB
        ),
    )(*in_hbm([left, right]))


def settle_kernel(own, near, far, regroup, out_ref):
    f32 = jnp.float32
    summed = own[...].astype(f32) + near[...].astype(f32) + far[...].astype(f32)
    out_ref[...] = t_matmul(regroup[...], summed.astype(jnp.bfloat16)).astype(jnp.bfloat16)


def finish_kernel(received, query_ref, key_ref, value_ref, output_ref, small_ref):
    f32 = jnp.float32
    width = query_ref.shape[1]
    total = received[0].astype(f32)
    for index in range(1, received.shape[0]):
        total = total + received[index].astype(f32)
    query_ref[...] = total[:, :width]
    key_ref[...] = total[:, width : 2 * width]
    value_ref[...] = total[:, 2 * width : 3 * width]
    output_ref[...] = total[:, 3 * width : 4 * width].T
    low = 4 * width
    lanes = small_ref.shape[1]
    small_ref[...] = (
        total[:, low : low + lanes] + total[:, low + HEAD_DIM : low + HEAD_DIM + lanes]
    )


def weight_blocks_kernel(query, key, value, router, gain1, bias1, gain2, bias2, out_ref):
    bf16 = jnp.bfloat16
    devices_on, seq_size, shard, lanes = out_ref.shape
    width = query.shape[1] // seq_size
    spots = lax.broadcasted_iota(jnp.int32, (8, shard), 0)
    vectors = jnp.zeros((8, shard), bf16)
    for index, vector in enumerate((gain1, bias1, gain2, bias2)):
        vectors = jnp.where(spots == index, vector[...], vectors)
    tail = lanes - 3 * width
    where_to = lax.broadcasted_iota(jnp.int32, (8, tail), 0) + EXPERTS
    placed = (lax.broadcasted_iota(jnp.int32, (8, tail), 1) == where_to).astype(bf16)
    rest = t_matmul(vectors, placed).astype(bf16)
    for part in range(seq_size):
        low = part * width
        for index, matrix in enumerate((query, key, value)):
            block = matrix[:, low : low + width]
            for copy in range(devices_on):
                out_ref[copy, part, :, index * width : (index + 1) * width] = block
        for copy in range(devices_on):
            out_ref[copy, part, :, 3 * width :] = rest
            out_ref[copy, part, :, 3 * width : 3 * width + EXPERTS] = router[...]


FAR = [(index, index ^ 2) for index in range(4)]
NEAR = [(index, index ^ 1) for index in range(4)]


def seq_gather(block):
    far = lax.ppermute(block, "seq", FAR)
    return (block, far, lax.ppermute(block, "seq", NEAR), lax.ppermute(far, "seq", NEAR))


def seq_reduce(own, far, near, diag):
    beside = lax.ppermute(diag, "seq", NEAR)
    pair = (far.astype(jnp.float32) + beside.astype(jnp.float32)).astype(far.dtype)
    return (own, lax.ppermute(near, "seq", NEAR), lax.ppermute(pair, "seq", FAR))


def body(
    block_in,
    expert_ids,
    ln1_gain,
    ln1_bias,
    w_query,
    w_key,
    w_value,
    w_output,
    ln2_gain,
    ln2_bias,
    w_router,
    w_expert_in,
    w_expert_out,
    cotangent,
):
    bf16 = jnp.bfloat16
    f32 = jnp.float32
    fsdp_size = lax.axis_size("fsdp")
    seq_size = lax.axis_size("seq")
    devices = fsdp_size * seq_size
    shard = w_query.shape[0]
    head_cols = D // seq_size
    local_slices = w_expert_in.shape[0]
    local_experts = max(1, local_slices // 2)
    halves = local_slices // local_experts
    copies = 2 // halves
    tokens_in = block_in[0]
    upstream = cotangent[0]
    chosen = expert_ids[0]
    token_count = chosen.shape[0]

    moves = [
        (fsdp_size * part + place, seq_size * place + part)
        for part in range(seq_size)
        for place in range(fsdp_size)
    ]
    w_out_rows = lax.ppermute(w_output, ("fsdp", "seq"), moves)
    w_out_rows = jnp.broadcast_to(w_out_rows, (fsdp_size, shard, D))
    w_out_rows = lax.all_to_all(w_out_rows, "fsdp", split_axis=0, concat_axis=0, tiled=True)
    w_out_rows = w_out_rows.reshape(head_cols, D)
    lanes = 3 * head_cols + EXPERTS + 4
    outer = fsdp_size // 2
    parity = lax.axis_index("fsdp") % 2
    sent = call(
        weight_blocks_kernel,
        [shaped(bf16, outer, seq_size, shard, lanes)],
        [w_query, w_key, w_value, w_router]
        + [v.reshape(1, shard) for v in (ln1_gain, ln1_bias, ln2_gain, ln2_bias)],
    )[0].reshape(devices // 2, shard, -1)
    groups = [
        [(2 * place + bit) * seq_size + part for place in range(outer) for part in range(seq_size)]
        for bit in range(2)
    ]
    held_own = lax.all_to_all(
        sent,
        ("fsdp", "seq"),
        split_axis=0,
        concat_axis=0,
        axis_index_groups=groups,
        tiled=True,
    )
    image_rows = seq_size * shard
    held_own = held_own.reshape(outer, image_rows, lanes)
    held_other = lax.ppermute(held_own, "fsdp", [(i, i ^ 1) for i in range(fsdp_size)])
    if image_rows % 16:
        pairs = jnp.stack([held_own, held_other], 1)
        pairs = jnp.where(parity == 0, pairs, pairs[:, ::-1]).reshape(2, 1, D // 2, lanes)
        held_own, held_other = pairs[0], pairs[1]
        parity = jnp.zeros((), jnp.int32)
    parity = parity.astype(jnp.int32).reshape(1)

    hot = (chosen.reshape(-1)[:, None] == jnp.arange(EXPERTS)[None, :]).astype(bf16)
    routes = token_count * TOP
    earlier = (jnp.arange(routes)[:, None] > jnp.arange(routes)[None, :]).astype(bf16)
    slot = jnp.sum(matmul(earlier, hot) * hot.astype(f32), 1).astype(jnp.int32)
    position = chosen * (CAP * copies) + slot.reshape(token_count, TOP)
    table_rows = EXPERTS * copies * CAP
    local_rows = local_experts * fsdp_size * CAP
    spot = jnp.arange(local_rows)
    source_of = (spot // CAP % fsdp_size) * (local_experts * CAP) + (
        spot // (CAP * fsdp_size) * CAP + spot % CAP
    )
    regroup = (source_of[:, None] == spot[None, :]).astype(bf16)

    def to_experts(table):
        table = table.reshape(fsdp_size, local_experts * CAP, D)
        received = lax.all_to_all(table, "fsdp", split_axis=0, concat_axis=0, tiled=True)
        grouped = matmul(regroup, received.reshape(local_rows, D)).astype(bf16)
        return seq_gather(grouped.reshape(local_experts, fsdp_size * CAP, D))

    def settle(partial, after):
        blocks = [part.reshape(local_rows, D) for part in seq_reduce(*partial)]
        return call(
            settle_kernel,
            [shaped(bf16, local_rows, D)],
            [*blocks, regroup],
            after=after,
            fresh=(1, 2),
            flops=2 * local_rows * local_rows * D,
        )[0]

    def from_experts(settled):
        returned = lax.all_to_all(
            settled.reshape(fsdp_size, local_experts * CAP, D),
            "fsdp",
            split_axis=0,
            concat_axis=0,
            tiled=True,
        )
        return returned.reshape(table_rows, D)

    normed_blocks = seq_gather(
        call(first_norm_kernel, [shaped(bf16, token_count, D)], [tokens_in])[0]
    )
    image = token_count * seq_size
    columns = 3 * head_cols
    normed_one, normed_in, qkv, head_mixed, logsum, vectors, held = call(
        attend_kernel,
        [
            shaped(bf16, image, D),
            shaped(bf16, image, D),
            shaped(bf16, image, columns),
            shaped(bf16, image, head_cols),
            shaped(f32, image, 8),
            shaped(f32, 8, D),
            shaped(bf16, held_own.shape[0], 2, *held_own.shape[1:]),
        ],
        [*normed_blocks, held_own, held_other, parity],
        fresh=(1, 2, 3, 4, 5),
        scalars=(6,),
        flops=6 * (2 * image * D * columns + 4 * image * image * head_cols),
    )
    held = held.reshape(D, lanes)
    router = held[:, columns : columns + EXPERTS]
    out_partial = matmul(head_mixed, w_out_rows).astype(bf16)
    out_blocks = [out_partial[i * token_count : (i + 1) * token_count] for i in range(seq_size)]

    residual, expert_rows, router_probs, rows_table = call(
        functools.partial(route_kernel, copies=copies),
        [
            shaped(f32, token_count, D),
            shaped(bf16, token_count, D),
            shaped(f32, token_count, EXPERTS),
            shaped(bf16, table_rows, D),
        ],
        [tokens_in, *seq_reduce(*out_blocks), vectors, router, position],
        fresh=(1, 2, 3, 6),
        light=True,
    )
    spots = jnp.arange(table_rows)[None, None, :] - position[:, :, None]
    hits = (spots == 0) if copies == 1 else ((spots == 0) | (spots == CAP))
    cots_table = t_matmul(jnp.any(hits, 1).astype(bf16), upstream.astype(bf16)).astype(bf16)
    slot_cots = to_experts(cots_table)
    slot_rows = to_experts(rows_table)

    first = (lax.axis_index("fsdp") * local_slices // 2).astype(jnp.int32).reshape(1)
    results = experts(
        first,
        slot_rows,
        slot_cots,
        router,
        w_expert_in,
        w_expert_out,
    )
    out_parts, grad_parts = results[:4], results[4:8]
    all_rows, all_cots, hidden_act, grad_inner, dots = results[8:]
    grad_expert_in = expert_products(all_rows, grad_inner)
    grad_expert_out = expert_products(hidden_act, all_cots)
    me = lax.axis_index("seq")
    turned = jnp.array([0, 2, 1, 3])[me ^ jnp.arange(seq_size)]
    dots = dots[:, :, 0].reshape(local_experts, seq_size, fsdp_size, CAP)
    dots = jnp.take(dots.transpose(2, 1, 0, 3), turned, axis=1)
    dots = lax.all_to_all(
        dots.reshape(devices, 1, local_experts * CAP),
        ("fsdp", "seq"),
        split_axis=0,
        concat_axis=0,
        tiled=True,
    )
    route_dots = jnp.sum(dots.reshape(fsdp_size, seq_size, -1), 1).reshape(1, table_rows)
    grad_table = from_experts(settle(grad_parts, [grad_expert_in]))
    grad_residual, grad_res_half, small_sums, out_settled = call(
        functools.partial(combine_kernel, copies=copies),
        [
            shaped(f32, token_count, D),
            shaped(bf16, token_count, D),
            shaped(f32, D, EXPERTS + 4),
            shaped(bf16, local_rows, D),
        ],
        [
            residual,
            upstream,
            vectors,
            router,
            expert_rows,
            router_probs,
            chosen,
            position,
            route_dots,
            grad_table,
            *[block.reshape(local_rows, D) for block in seq_reduce(*out_parts)],
            regroup,
        ],
        after=[grad_expert_out],
        fresh=(6, 7, 8, 9, 11, 12),
    )

    out_table = from_experts(out_settled)
    block_out = call(
        functools.partial(block_out_kernel, copies=copies),
        [shaped(f32, token_count, D)],
        [residual, router_probs, chosen, position, out_table],
        fresh=(2, 3, 4),
    )[0]

    *gn_parts, grad_weights = call(
        attend_back_kernel,
        [shaped(bf16, token_count, D)] * 4
        + [shaped(bf16, D, 4 * head_cols + 2 * HEAD_DIM)],
        [
            *seq_gather(grad_res_half),
            w_out_rows,
            held,
            qkv,
            head_mixed,
            logsum,
            normed_one,
            normed_in,
            small_sums,
        ],
        fresh=(1, 2, 3, 4),
        scratch=[pltpu.VMEM((image, D), bf16), pltpu.VMEM((image, columns), bf16)],
        flops=4 * (4 * image * D * 4 * head_cols + 10 * image * image * head_cols),
    )
    grad_weights = held_back(grad_weights, out_table)
    grad_weights = lax.all_to_all(
        grad_weights.reshape(fsdp_size, D // fsdp_size, 4 * head_cols + 2 * HEAD_DIM),
        "fsdp",
        split_axis=0,
        concat_axis=0,
        tiled=True,
    )
    *grad_squares, small_sums = call(
        finish_kernel,
        [shaped(f32, D // fsdp_size, head_cols)] * 3
        + [shaped(f32, head_cols, D // fsdp_size), shaped(f32, D // fsdp_size, EXPERTS + 4)],
        [grad_weights],
        after=[block_out],
        fresh=(0,),
    )
    place = lax.axis_index("seq")
    for step, swap in ((2, FAR), (1, NEAR)):
        rows = small_sums.shape[0] // 2
        upper = (place // step) % 2
        away = lax.dynamic_slice_in_dim(small_sums, (1 - upper) * rows, rows)
        kept = lax.dynamic_slice_in_dim(small_sums, upper * rows, rows)
        small_sums = kept + lax.ppermute(away, "seq", swap)
    own, near, far = seq_reduce(*gn_parts)
    own_grad_normed = own.astype(f32) + near.astype(f32) + far.astype(f32)
    own_normed, own_inverse = norm_forward(tokens_in)
    grad_tokens = grad_residual + norm_backward(
        own_grad_normed * vectors[0], own_normed, own_inverse
    )
    return (
        block_out[None],
        grad_tokens[None],
        small_sums[:, EXPERTS],
        small_sums[:, EXPERTS + 1],
        *grad_squares,
        small_sums[:, EXPERTS + 2],
        small_sums[:, EXPERTS + 3],
        small_sums[:, :EXPERTS],
        grad_expert_in,
        grad_expert_out,
    )


def solution(mesh):
    return jax.shard_map(
        body,
        mesh=mesh,
        in_specs=(
            P("fsdp", "seq", None),
            P("fsdp", "seq", None),
            P(("fsdp", "seq")),
            P(("fsdp", "seq")),
            P(("fsdp", "seq"), None),
            P(("fsdp", "seq"), None),
            P(("fsdp", "seq"), None),
            P(("fsdp", "seq"), None),
            P(("fsdp", "seq")),
            P(("fsdp", "seq")),
            P(("fsdp", "seq"), None),
            P("fsdp", None, "seq"),
            P("fsdp", "seq", None),
            P("fsdp", "seq", None),
        ),
        out_specs=(
            P("fsdp", "seq", None),
            P("fsdp", "seq", None),
            P(("fsdp", "seq")),
            P(("fsdp", "seq")),
            P("fsdp", "seq"),
            P("fsdp", "seq"),
            P("fsdp", "seq"),
            P("seq", "fsdp"),
            P(("fsdp", "seq")),
            P(("fsdp", "seq")),
            P(("fsdp", "seq"), None),
            P("fsdp", None, "seq"),
            P("fsdp", "seq", None),
        ),
        check_vma=False,
    )
```

```python
import functools

import jax
import jax.numpy as jnp
from jax import lax
from jax.experimental import pallas as pl
from jax.experimental.pallas import tpu as pltpu
from jax.sharding import PartitionSpec as P

D = 768
HEAD_DIM = 64
EXPERTS = 32
TOP = 2
CAP = 10


EPS = 1e-06
TANH_SCALE = 0.7978845608028654
CUBIC = 0.044715


def matmul(left_side, right_side):
    return jnp.dot(left_side, right_side, preferred_element_type=jnp.float32)


def matmul_t(left_side, right_side):
    return lax.dot_general(
        left_side, right_side, (((1,), (1,)), ((), ())), preferred_element_type=jnp.float32
    )


def t_matmul(left_side, right_side):
    return lax.dot_general(
        left_side, right_side, (((0,), (0,)), ((), ())), preferred_element_type=jnp.float32
    )


def norm_forward(values):
    centre = values - jnp.mean(values, -1, keepdims=True)
    inverse = lax.rsqrt(jnp.mean(centre * centre, -1, keepdims=True) + EPS)
    return (centre * inverse, inverse)


def norm_backward(grad_normed, normed, inverse):
    return inverse * (
        grad_normed
        - jnp.mean(grad_normed, -1, keepdims=True)
        - normed * jnp.mean(grad_normed * normed, -1, keepdims=True)
    )


def gelu_both(inner_act):
    square = inner_act * inner_act
    bent = jnp.tanh(TANH_SCALE * inner_act * (1.0 + CUBIC * square))
    value = 0.5 * inner_act * (1.0 + bent)
    slope = 0.5 * (1.0 + bent) + 0.5 * inner_act * (1.0 - bent * bent) * TANH_SCALE * (
        1.0 + 3.0 * CUBIC * square
    )
    return (value, slope)


SCALING = HEAD_DIM ** (-0.5)
MIB = 1024 * 1024
WHOLE = pl.BlockSpec(memory_space=pltpu.VMEM)


def call(kernel, outputs, operands, after=(), fresh=(), scalars=(), scratch=(), flops=0, mib=20, light=False):
    moved = 0 if light else sum(v.size * v.dtype.itemsize for v in operands)
    used = len(operands)

    def inner(*refs):
        kernel(*refs[:used], *refs[used + len(after) :])

    operands = [
        operand if index in fresh or index in scalars else in_hbm([operand])[0]
        for index, operand in enumerate(operands)
    ] + in_hbm(after)
    return pl.pallas_call(
        inner,
        out_shape=outputs,
        in_specs=[
            pl.BlockSpec(memory_space=pltpu.SMEM) if index in scalars else WHOLE
            for index in range(used)
        ]
        + [pl.BlockSpec(memory_space=pl.ANY)] * len(after),
        out_specs=[WHOLE] * len(outputs),
        scratch_shapes=scratch,
        cost_estimate=pl.CostEstimate(flops=flops, bytes_accessed=moved, transcendentals=0),
        compiler_params=pltpu.CompilerParams(vmem_limit_bytes=mib * MIB),
    )(*operands)


def shaped(dtype, *shape):
    return pltpu.HBM(shape, dtype)


def in_hbm(operands):
    return [pltpu.with_memory_space_constraint(operand, pltpu.HBM) for operand in operands]


def held_back(array, other):
    anywhere = pl.BlockSpec(memory_space=pl.ANY)
    return pl.pallas_call(
        lambda array_ref, other_ref, out_ref: None,
        out_shape=shaped(array.dtype, *array.shape),
        in_specs=[anywhere, anywhere],
        out_specs=anywhere,
        input_output_aliases={0: 0},
    )(*in_hbm([array]), other)


def first_norm_kernel(tokens, normed_ref):
    normed_ref[...] = norm_forward(tokens[...])[0].astype(jnp.bfloat16)


def attend_kernel(
    own, far, near, diag, held_own, held_other, parity,
    normed_ref, normed_in_ref, qkv_ref, mixed_ref, logsum_ref, vec_ref, held_ref, router_ref
):
    bf16 = jnp.bfloat16
    f32 = jnp.float32
    columns = qkv_ref.shape[1]
    outer, _, rows, lanes = held_ref.shape
    bit = parity[0]
    for place in range(outer):
        held_ref[place, bit] = held_own[place]
        held_ref[place, 1 - bit] = held_other[place]
    held = held_ref[...].reshape(outer * 2 * rows, lanes)
    wanted = lax.broadcasted_iota(jnp.int32, (8, lanes), 0) + (columns + EXPERTS)
    picker = (lax.broadcasted_iota(jnp.int32, (8, lanes), 1) == wanted).astype(bf16)
    router_ref[...] = held[:, columns : columns + EXPERTS]
    vectors = matmul_t(picker, held)
    vec_ref[...] = vectors
    count = own.shape[0]
    for index, block in enumerate((own, far, near, diag)):
        normed = block[...].astype(f32)
        rows = pl.ds(index * count, count)
        normed_ref[rows, :] = block[...]
        normed_in_ref[rows, :] = (normed * vectors[0:1] + vectors[1:2]).astype(bf16)
    qkv_ref[...] = matmul(normed_in_ref[...], held[:, :columns]).astype(bf16)
    width = columns // 3
    logsum_ref[...] = jnp.zeros_like(logsum_ref)
    for low in range(0, width, HEAD_DIM):
        query = qkv_ref[:, low : low + HEAD_DIM]
        key = qkv_ref[:, width + low : width + low + HEAD_DIM]
        value = qkv_ref[:, 2 * width + low : 2 * width + low + HEAD_DIM]
        scores = matmul_t(query, key) * SCALING
        highest = jnp.max(scores, -1, keepdims=True)
        raised = jnp.exp(scores - highest)
        total = jnp.sum(raised, -1, keepdims=True)
        head = low // HEAD_DIM
        logsum_ref[:, head : head + 1] = highest + jnp.log(total)
        weights = (raised * (1.0 / total)).astype(bf16)
        mixed_ref[:, low : low + HEAD_DIM] = matmul(weights, value).astype(bf16)


def attend_back_kernel(
    own,
    far,
    near,
    diag,
    w_out,
    held,
    qkv,
    mixed,
    logsum,
    normed,
    normed_in,
    small,
    gn_own,
    gn_far,
    gn_near,
    gn_diag,
    dw_ref,
    gr_ref,
    gqkv_ref,
):
    bf16 = jnp.bfloat16
    f32 = jnp.float32
    count = own.shape[0]
    columns = qkv.shape[1]
    width = columns // 3
    for index, block in enumerate((own, far, near, diag)):
        gr_ref[pl.ds(index * count, count), :] = block[...]
    grad_mixed = matmul_t(gr_ref[...], w_out[...]).astype(bf16)
    for low in range(0, width, HEAD_DIM):
        head = low // HEAD_DIM
        query = qkv[:, low : low + HEAD_DIM]
        key = qkv[:, width + low : width + low + HEAD_DIM]
        value = qkv[:, 2 * width + low : 2 * width + low + HEAD_DIM]
        grad_head = grad_mixed[:, low : low + HEAD_DIM]
        delta = jnp.sum(
            grad_head.astype(f32) * mixed[:, low : low + HEAD_DIM].astype(f32), -1, keepdims=True
        )
        probs = jnp.exp(matmul_t(query, key) * SCALING - logsum[:, head : head + 1])
        grad_probs = matmul_t(grad_head, value)
        grad_scores = (probs * (grad_probs - delta) * SCALING).astype(bf16)
        gqkv_ref[:, low : low + HEAD_DIM] = matmul(grad_scores, key).astype(bf16)
        gqkv_ref[:, width + low : width + low + HEAD_DIM] = t_matmul(grad_scores, query).astype(
            bf16
        )
        gqkv_ref[:, 2 * width + low : 2 * width + low + HEAD_DIM] = t_matmul(
            probs.astype(bf16), grad_head
        ).astype(bf16)
    grad_normed = matmul_t(gqkv_ref[...], held[:, :columns])
    for index, block in enumerate((gn_own, gn_far, gn_near, gn_diag)):
        block[...] = grad_normed[index * count : (index + 1) * count].astype(bf16)
    dw_ref[:, :columns] = t_matmul(normed_in[...], gqkv_ref[...]).astype(bf16)
    dw_ref[:, columns : columns + width] = t_matmul(gr_ref[...], mixed[...]).astype(bf16)
    gain_row = jnp.sum(grad_normed * normed[...].astype(f32), 0, keepdims=True)
    bias_row = jnp.sum(grad_normed, 0, keepdims=True)
    row = lax.broadcasted_iota(jnp.int32, (8, gain_row.shape[1]), 0)
    both = jnp.where(row == 0, gain_row, jnp.where(row == 1, bias_row, 0.0))
    sums = small[...] + columns_of(both, EXPERTS, small.shape[1])
    high = sums.astype(bf16)
    low = columns + width
    dw_ref[:, low:] = jnp.zeros((dw_ref.shape[0], dw_ref.shape[1] - low), bf16)
    dw_ref[:, low : low + sums.shape[1]] = high
    dw_ref[:, low + HEAD_DIM : low + HEAD_DIM + sums.shape[1]] = (
        sums - high.astype(f32)
    ).astype(bf16)


def columns_of(rows, first, lanes):
    count = rows.shape[0]
    spots = lax.broadcasted_iota(jnp.int32, (count, lanes), 1)
    placed = (spots == lax.broadcasted_iota(jnp.int32, (count, lanes), 0) + first).astype(
        jnp.float32
    )
    return lax.dot_general(
        rows,
        placed,
        (((0,), (0,)), ((), ())),
        preferred_element_type=jnp.float32,
        precision=lax.Precision.HIGHEST,
    )


def picks_of(position, choice, rows, copies):
    spots = lax.broadcasted_iota(jnp.int32, (position.shape[0], rows), 1)
    first = position[:, choice : choice + 1]
    hit = spots == first
    for copy in range(1, copies):
        hit = hit | (spots == first + copy * CAP)
    return hit.astype(jnp.float32)


def gates_of(probs, chosen, choice):
    spots = lax.broadcasted_iota(jnp.int32, probs.shape, 1)
    return jnp.sum(
        jnp.where(spots == chosen[:, choice : choice + 1], probs, 0.0), -1, keepdims=True
    )


def route_kernel(
    tokens_in, own, near, far, vectors, router, position, residual_ref, rows_ref, probs_ref, table_ref,
    *, copies
):
    bf16 = jnp.bfloat16
    f32 = jnp.float32
    residual = tokens_in[...] + (
        own[...].astype(f32) + near[...].astype(f32) + far[...].astype(f32)
    )
    residual_ref[...] = residual
    normed, _ = norm_forward(residual)
    rows = (normed * vectors[2:3, :] + vectors[3:4, :]).astype(bf16)
    rows_ref[...] = rows
    logits = matmul(rows, router[...])
    raised = jnp.exp(logits - jnp.max(logits, -1, keepdims=True))
    probs_ref[...] = raised / jnp.sum(raised, -1, keepdims=True)
    size = table_ref.shape[0]
    spots = picks_of(position[...], 0, size, copies) + picks_of(position[...], 1, size, copies)
    table_ref[...] = t_matmul(spots.astype(bf16), rows).astype(bf16)


def combine_kernel(
    residual, upstream, vectors, router, rows, probs, chosen, position, route_dots, table,
    own, near, far, regroup,
    grad_ref, half_ref, small_ref, settled_ref, *, copies
):
    bf16 = jnp.bfloat16
    f32 = jnp.float32
    size = table.shape[0]
    picks = [picks_of(position[...], choice, size, copies) for choice in range(TOP)]
    grad_probs = jnp.zeros(probs.shape, f32)
    spots = lax.broadcasted_iota(jnp.int32, probs.shape, 1)
    for choice in range(TOP):
        grad_gate = jnp.sum(picks[choice] * route_dots[0:1, :], -1, keepdims=True)
        grad_probs = grad_probs + jnp.where(
            spots == chosen[:, choice : choice + 1], grad_gate, 0.0
        )
    shares = probs[...]
    grad_logits = shares * (grad_probs - jnp.sum(shares * grad_probs, -1, keepdims=True))
    grad_logits = grad_logits.astype(bf16)
    grad_rows = matmul((picks[0] + picks[1]).astype(bf16), table[...]) + matmul_t(
        grad_logits, router[...]
    )
    normed, inverse = norm_forward(residual[...])
    grad = upstream[...] + norm_backward(grad_rows * vectors[2:3, :], normed, inverse)
    grad_ref[...] = grad
    half_ref[...] = grad.astype(bf16)
    gain_row = jnp.sum(grad_rows * normed, 0, keepdims=True)
    bias_row = jnp.sum(grad_rows, 0, keepdims=True)
    row = lax.broadcasted_iota(jnp.int32, (8, gain_row.shape[1]), 0)
    both = jnp.where(row == 0, gain_row, jnp.where(row == 1, bias_row, 0.0))
    lanes = small_ref.shape[1]
    small_ref[...] = columns_of(both, EXPERTS + 2, lanes)
    small_ref[:, :EXPERTS] = t_matmul(rows[...], grad_logits)
    settle_kernel(own, near, far, regroup, settled_ref)


def block_out_kernel(residual, probs, chosen, position, table, out_ref, *, copies):
    out = residual[...]
    for choice in range(TOP):
        pick = picks_of(position[...], choice, table.shape[0], copies).astype(jnp.bfloat16)
        out = out + gates_of(probs[...], chosen, choice) * matmul(pick, table[...])
    out_ref[...] = out


def expert_kernel(
    first,
    x_own, x_far, x_near, x_diag,
    c_own, c_far, c_near, c_diag,
    router, w_in, w_out,
    o_own, o_far, o_near, o_diag,
    g_own, g_far, g_near, g_diag,
    rows_ref, cots_ref, hidden_ref, inner_ref, dots_ref,
):
    bf16 = jnp.bfloat16
    f32 = jnp.float32
    count = x_own.shape[1]
    parts = [pl.ds(index * count, count) for index in range(4)]
    for part, block, cots in zip(
        parts, (x_own, x_far, x_near, x_diag), (c_own, c_far, c_near, c_diag)
    ):
        rows_ref[0, part, :] = block[0]
        cots_ref[0, part, :] = cots[0]
    rows = rows_ref[0]
    bare = cots_ref[0]
    logits = matmul(rows, router[...])
    raised = jnp.exp(logits - jnp.max(logits, -1, keepdims=True))
    wanted = first[0] + pl.program_id(0)
    spots = lax.broadcasted_iota(jnp.int32, logits.shape, 1)
    gate = jnp.sum(jnp.where(spots == wanted, raised, 0.0), -1, keepdims=True) / jnp.sum(
        raised, -1, keepdims=True
    )
    cots = (gate * bare.astype(f32)).astype(bf16)
    cots_ref[0] = cots
    out_sum = None
    for half in range(w_in.shape[0]):
        value, slope = gelu_both(matmul(rows, w_in[half]))
        hidden = value.astype(bf16)
        hidden_ref[half] = hidden
        inner = (matmul_t(cots, w_out[half]) * slope).astype(bf16)
        inner_ref[half] = inner
        out = matmul(hidden, w_out[half])
        grad = matmul_t(inner, w_in[half])
        out_sum = out if out_sum is None else out_sum + out
        grad_sum = grad if half == 0 else grad_sum + grad
    dots = jnp.sum(out_sum * bare.astype(f32), -1, keepdims=True)
    dots_ref[0] = jnp.broadcast_to(dots, dots_ref.shape[1:])
    for index, (out, grad) in enumerate(
        zip((o_own, o_far, o_near, o_diag), (g_own, g_far, g_near, g_diag))
    ):
        low = index * count
        out[0] = out_sum[low : low + count].astype(bf16)
        grad[0] = grad_sum[low : low + count].astype(bf16)


def experts(first, rows, cots, router, w_in, w_out):
    bf16 = jnp.bfloat16
    f32 = jnp.float32
    local_experts, count, _ = rows[0].shape
    slices, _, hidden_cols = w_in.shape
    halves = slices // local_experts
    total = 4 * count
    by_expert = pl.BlockSpec((1, count, D), lambda e: (e, 0, 0))
    by_expert_all = pl.BlockSpec((1, total, D), lambda e: (e, 0, 0))
    by_slice = lambda *shape: pl.BlockSpec((halves,) + shape, lambda e: (e, 0, 0))
    flops = 8 * slices * total * D * hidden_cols
    moved = 4 * slices * D * hidden_cols + 12 * local_experts * total * D
    return pl.pallas_call(
        expert_kernel,
        grid=(local_experts,),
        in_specs=[pl.BlockSpec(memory_space=pltpu.SMEM)]
        + [by_expert] * 8
        + [
            pl.BlockSpec((D, EXPERTS), lambda e: (0, 0)),
            by_slice(D, hidden_cols),
            by_slice(hidden_cols, D),
        ],
        out_specs=[by_expert] * 8
        + [
            by_expert_all,
            by_expert_all,
            by_slice(total, hidden_cols),
            by_slice(total, hidden_cols),
            pl.BlockSpec((1, total, 8), lambda e: (e, 0, 0)),
        ],
        out_shape=[shaped(bf16, local_experts, count, D)] * 8
        + [shaped(bf16, local_experts, total, D)] * 2
        + [shaped(bf16, slices, total, hidden_cols)] * 2
        + [shaped(f32, local_experts, total, 8)],
        cost_estimate=pl.CostEstimate(flops=flops, bytes_accessed=moved, transcendentals=0),
        compiler_params=pltpu.CompilerParams(
            vmem_limit_bytes=(28 if count <= 128 else 58) * MIB
        ),
    )(first, *rows, *cots, router, *in_hbm([w_in, w_out]))


def product_kernel(left, right, *rest):
    out_ref = rest[-1]
    for index in range(out_ref.shape[0]):
        out_ref[index] = t_matmul(
            left[min(index, left.shape[0] - 1)], right[min(index, right.shape[0] - 1)]
        )


def expert_products(left, right, after=()):
    slices = max(left.shape[0], right.shape[0])
    local_experts = min(left.shape[0], right.shape[0])
    shape = (left.shape[2], right.shape[2])
    block = lambda first, *rest: pl.BlockSpec((first // local_experts,) + rest, lambda e: (e, 0, 0))
    flops = 2 * slices * left.shape[1] * shape[0] * shape[1]
    return pl.pallas_call(
        product_kernel,
        grid=(local_experts,),
        in_specs=[block(*left.shape), block(*right.shape)]
        + [pl.BlockSpec(memory_space=pl.ANY)] * len(after),
        out_specs=block(slices, *shape),
        out_shape=shaped(jnp.float32, slices, *shape),
        cost_estimate=pl.CostEstimate(
            flops=flops,
            bytes_accessed=4 * slices * shape[0] * shape[1] + 2 * (left.size + right.size),
            transcendentals=0,
        ),
        compiler_params=pltpu.CompilerParams(
            vmem_limit_bytes=(16 if left.shape[1] <= 512 else 48) * MIB
        ),
    )(*in_hbm([left, right, *after]))


def settle_kernel(own, near, far, regroup, out_ref):
    f32 = jnp.float32
    summed = own[...].astype(f32) + near[...].astype(f32) + far[...].astype(f32)
    out_ref[...] = t_matmul(regroup[...], summed.astype(jnp.bfloat16)).astype(jnp.bfloat16)


def finish_kernel(received, query_ref, key_ref, value_ref, output_ref, small_ref):
    f32 = jnp.float32
    width = query_ref.shape[1]
    total = received[0].astype(f32)
    for index in range(1, received.shape[0]):
        total = total + received[index].astype(f32)
    query_ref[...] = total[:, :width]
    key_ref[...] = total[:, width : 2 * width]
    value_ref[...] = total[:, 2 * width : 3 * width]
    output_ref[...] = total[:, 3 * width : 4 * width].T
    low = 4 * width
    lanes = small_ref.shape[1]
    small_ref[...] = (
        total[:, low : low + lanes] + total[:, low + HEAD_DIM : low + HEAD_DIM + lanes]
    )


def weight_blocks_kernel(query, key, value, router, gain1, bias1, gain2, bias2, out_ref):
    bf16 = jnp.bfloat16
    devices_on, seq_size, shard, lanes = out_ref.shape
    width = query.shape[1] // seq_size
    spots = lax.broadcasted_iota(jnp.int32, (8, shard), 0)
    vectors = jnp.zeros((8, shard), bf16)
    for index, vector in enumerate((gain1, bias1, gain2, bias2)):
        vectors = jnp.where(spots == index, vector[...], vectors)
    tail = lanes - 3 * width
    where_to = lax.broadcasted_iota(jnp.int32, (8, tail), 0) + EXPERTS
    placed = (lax.broadcasted_iota(jnp.int32, (8, tail), 1) == where_to).astype(bf16)
    rest = t_matmul(vectors, placed).astype(bf16)
    for part in range(seq_size):
        low = part * width
        for index, matrix in enumerate((query, key, value)):
            block = matrix[:, low : low + width]
            for copy in range(devices_on):
                out_ref[copy, part, :, index * width : (index + 1) * width] = block
        for copy in range(devices_on):
            out_ref[copy, part, :, 3 * width :] = rest
            out_ref[copy, part, :, 3 * width : 3 * width + EXPERTS] = router[...]


FAR = [(index, index ^ 2) for index in range(4)]
NEAR = [(index, index ^ 1) for index in range(4)]
ACROSS = [(index, index ^ 3) for index in range(4)]


def seq_gather(block):
    far = lax.ppermute(block, "seq", FAR)
    return (block, far, lax.ppermute(block, "seq", NEAR), lax.ppermute(far, "seq", NEAR))


def seq_reduce(own, far, near, diag):
    beside = lax.ppermute(diag, "seq", NEAR)
    pair = (far.astype(jnp.float32) + beside.astype(jnp.float32)).astype(far.dtype)
    return (own, lax.ppermute(near, "seq", NEAR), lax.ppermute(pair, "seq", FAR))


def body(
    block_in,
    expert_ids,
    ln1_gain,
    ln1_bias,
    w_query,
    w_key,
    w_value,
    w_output,
    ln2_gain,
    ln2_bias,
    w_router,
    w_expert_in,
    w_expert_out,
    cotangent,
):
    bf16 = jnp.bfloat16
    f32 = jnp.float32
    fsdp_size = lax.axis_size("fsdp")
    seq_size = lax.axis_size("seq")
    devices = fsdp_size * seq_size
    shard = w_query.shape[0]
    head_cols = D // seq_size
    local_slices = w_expert_in.shape[0]
    local_experts = max(1, local_slices // 2)
    halves = local_slices // local_experts
    copies = 2 // halves
    tokens_in = block_in[0]
    upstream = cotangent[0]
    chosen = expert_ids[0]
    token_count = chosen.shape[0]

    moves = [
        (fsdp_size * part + place, seq_size * place + part)
        for part in range(seq_size)
        for place in range(fsdp_size)
    ]
    w_out_rows = lax.ppermute(w_output, ("fsdp", "seq"), moves)
    w_out_rows = jnp.broadcast_to(w_out_rows, (fsdp_size, shard, D))
    w_out_rows = lax.all_to_all(w_out_rows, "fsdp", split_axis=0, concat_axis=0, tiled=True)
    w_out_rows = w_out_rows.reshape(head_cols, D)
    lanes = 3 * head_cols + EXPERTS + 4
    outer = fsdp_size // 2
    parity = lax.axis_index("fsdp") % 2
    sent = call(
        weight_blocks_kernel,
        [shaped(bf16, outer, seq_size, shard, lanes)],
        [w_query, w_key, w_value, w_router]
        + [v.reshape(1, shard) for v in (ln1_gain, ln1_bias, ln2_gain, ln2_bias)],
    )[0].reshape(devices // 2, shard, -1)
    groups = [
        [(2 * place + bit) * seq_size + part for place in range(outer) for part in range(seq_size)]
        for bit in range(2)
    ]
    held_own = lax.all_to_all(
        sent,
        ("fsdp", "seq"),
        split_axis=0,
        concat_axis=0,
        axis_index_groups=groups,
        tiled=True,
    )
    image_rows = seq_size * shard
    held_own = held_own.reshape(outer, image_rows, lanes)
    held_other = lax.ppermute(held_own, "fsdp", [(i, i ^ 1) for i in range(fsdp_size)])
    if image_rows % 16:
        pairs = jnp.stack([held_own, held_other], 1)
        pairs = jnp.where(parity == 0, pairs, pairs[:, ::-1]).reshape(2, 1, D // 2, lanes)
        held_own, held_other = pairs[0], pairs[1]
        parity = jnp.zeros((), jnp.int32)
    parity = parity.astype(jnp.int32).reshape(1)

    hot = (chosen.reshape(-1)[:, None] == jnp.arange(EXPERTS)[None, :]).astype(bf16)
    routes = token_count * TOP
    earlier = (jnp.arange(routes)[:, None] > jnp.arange(routes)[None, :]).astype(bf16)
    slot = jnp.sum(matmul(earlier, hot) * hot.astype(f32), 1).astype(jnp.int32)
    position = chosen * (CAP * copies) + slot.reshape(token_count, TOP)
    table_rows = EXPERTS * copies * CAP
    local_rows = local_experts * fsdp_size * CAP
    spot = jnp.arange(local_rows)
    source_of = (spot // CAP % fsdp_size) * (local_experts * CAP) + (
        spot // (CAP * fsdp_size) * CAP + spot % CAP
    )
    regroup = (source_of[:, None] == spot[None, :]).astype(bf16)

    def to_experts(table):
        table = table.reshape(fsdp_size, local_experts * CAP, D)
        received = lax.all_to_all(table, "fsdp", split_axis=0, concat_axis=0, tiled=True)
        grouped = matmul(regroup, received.reshape(local_rows, D)).astype(bf16)
        return seq_gather(grouped.reshape(local_experts, fsdp_size * CAP, D))

    def settle(partial, after):
        blocks = [part.reshape(local_rows, D) for part in seq_reduce(*partial)]
        return call(
            settle_kernel,
            [shaped(bf16, local_rows, D)],
            [*blocks, regroup],
            after=after,
            fresh=(1, 2),
            flops=2 * local_rows * local_rows * D,
        )[0]

    def from_experts(settled):
        returned = lax.all_to_all(
            settled.reshape(fsdp_size, local_experts * CAP, D),
            "fsdp",
            split_axis=0,
            concat_axis=0,
            tiled=True,
        )
        return returned.reshape(table_rows, D)

    normed_blocks = seq_gather(
        call(first_norm_kernel, [shaped(bf16, token_count, D)], [tokens_in])[0]
    )
    image = token_count * seq_size
    columns = 3 * head_cols
    normed_one, normed_in, qkv, head_mixed, logsum, vectors, held, router = call(
        attend_kernel,
        [
            shaped(bf16, image, D),
            shaped(bf16, image, D),
            shaped(bf16, image, columns),
            shaped(bf16, image, head_cols),
            shaped(f32, image, 8),
            shaped(f32, 8, D),
            shaped(bf16, held_own.shape[0], 2, *held_own.shape[1:]),
            shaped(bf16, D, EXPERTS),
        ],
        [*normed_blocks, held_own, held_other, parity],
        fresh=(1, 2, 3, 4, 5),
        scalars=(6,),
        flops=3 * (2 * image * D * columns + 4 * image * image * head_cols),
    )
    held = held.reshape(D, lanes)
    out_partial = matmul(head_mixed, w_out_rows).astype(bf16)
    out_blocks = [out_partial[i * token_count : (i + 1) * token_count] for i in range(seq_size)]

    residual, expert_rows, router_probs, rows_table = call(
        functools.partial(route_kernel, copies=copies),
        [
            shaped(f32, token_count, D),
            shaped(bf16, token_count, D),
            shaped(f32, token_count, EXPERTS),
            shaped(bf16, table_rows, D),
        ],
        [tokens_in, *seq_reduce(*out_blocks), vectors, router, position],
        fresh=(1, 2, 3, 6),
        light=True,
    )
    spots = jnp.arange(table_rows)[None, None, :] - position[:, :, None]
    hits = (spots == 0) if copies == 1 else ((spots == 0) | (spots == CAP))
    cots_table = t_matmul(jnp.any(hits, 1).astype(bf16), upstream.astype(bf16)).astype(bf16)
    slot_cots = to_experts(cots_table)
    slot_rows = to_experts(rows_table)

    first = (lax.axis_index("fsdp") * local_slices // 2).astype(jnp.int32).reshape(1)
    results = experts(
        first,
        slot_rows,
        slot_cots,
        router,
        w_expert_in,
        w_expert_out,
    )
    out_parts, grad_parts = results[:4], results[4:8]
    all_rows, all_cots, hidden_act, grad_inner, dots = results[8:]
    grad_expert_out = expert_products(hidden_act, all_cots)
    me = lax.axis_index("seq")
    turned = jnp.array([0, 2, 1, 3])[me ^ jnp.arange(seq_size)]
    dots = dots[:, :, 0].reshape(local_experts, seq_size, fsdp_size, CAP)
    dots = jnp.take(dots.transpose(2, 1, 0, 3), turned, axis=1)
    dots = lax.all_to_all(
        dots.reshape(devices, 1, local_experts * CAP),
        ("fsdp", "seq"),
        split_axis=0,
        concat_axis=0,
        tiled=True,
    )
    route_dots = jnp.sum(dots.reshape(fsdp_size, seq_size, -1), 1).reshape(1, table_rows)
    grad_table = from_experts(settle(grad_parts, []))
    grad_residual, grad_res_half, small_sums, out_settled = call(
        functools.partial(combine_kernel, copies=copies),
        [
            shaped(f32, token_count, D),
            shaped(bf16, token_count, D),
            shaped(f32, D, EXPERTS + 4),
            shaped(bf16, local_rows, D),
        ],
        [
            residual,
            upstream,
            vectors,
            router,
            expert_rows,
            router_probs,
            chosen,
            position,
            route_dots,
            grad_table,
            *[block.reshape(local_rows, D) for block in seq_reduce(*out_parts)],
            regroup,
        ],
        after=[grad_expert_out],
        fresh=(6, 7, 8, 9, 11, 12),
    )

    out_table = from_experts(out_settled)
    block_out = call(
        functools.partial(block_out_kernel, copies=copies),
        [shaped(f32, token_count, D)],
        [residual, router_probs, chosen, position, out_table],
        fresh=(2, 3, 4),
    )[0]

    *gn_parts, grad_weights = call(
        attend_back_kernel,
        [shaped(bf16, token_count, D)] * 4
        + [shaped(bf16, D, 4 * head_cols + 2 * HEAD_DIM)],
        [
            *seq_gather(grad_res_half),
            w_out_rows,
            held,
            qkv,
            head_mixed,
            logsum,
            normed_one,
            normed_in,
            small_sums,
        ],
        fresh=(1, 2, 3, 4),
        scratch=[pltpu.VMEM((image, D), bf16), pltpu.VMEM((image, columns), bf16)],
        flops=4 * (4 * image * D * 4 * head_cols + 10 * image * image * head_cols),
    )
    grad_weights = held_back(grad_weights, out_table)
    grad_weights = lax.all_to_all(
        grad_weights.reshape(fsdp_size, D // fsdp_size, 4 * head_cols + 2 * HEAD_DIM),
        "fsdp",
        split_axis=0,
        concat_axis=0,
        tiled=True,
    )
    own, near, far = seq_reduce(*gn_parts)
    grad_expert_in = expert_products(all_rows, grad_inner, [far])
    *grad_squares, small_sums = call(
        finish_kernel,
        [shaped(f32, D // fsdp_size, head_cols)] * 3
        + [shaped(f32, head_cols, D // fsdp_size), shaped(f32, D // fsdp_size, EXPERTS + 4)],
        [grad_weights],
        after=[block_out, grad_expert_in],
        fresh=(0,),
    )
    pieces = []
    for step, swap in ((0, None), (2, FAR), (1, NEAR), (3, ACROSS)):
        piece = lax.dynamic_slice_in_dim(small_sums, (me ^ step) * shard, shard)
        pieces.append(piece if swap is None else lax.ppermute(piece, "seq", swap))
    small_sums = (pieces[0] + pieces[1]) + (pieces[2] + pieces[3])
    own_grad_normed = own.astype(f32) + near.astype(f32) + far.astype(f32)
    own_normed, own_inverse = norm_forward(tokens_in)
    grad_tokens = grad_residual + norm_backward(
        own_grad_normed * vectors[0], own_normed, own_inverse
    )
    return (
        block_out[None],
        grad_tokens[None],
        small_sums[:, EXPERTS],
        small_sums[:, EXPERTS + 1],
        *grad_squares,
        small_sums[:, EXPERTS + 2],
        small_sums[:, EXPERTS + 3],
        small_sums[:, :EXPERTS],
        grad_expert_in,
        grad_expert_out,
    )


def solution(mesh):
    return jax.shard_map(
        body,
        mesh=mesh,
        in_specs=(
            P("fsdp", "seq", None),
            P("fsdp", "seq", None),
            P(("fsdp", "seq")),
            P(("fsdp", "seq")),
            P(("fsdp", "seq"), None),
            P(("fsdp", "seq"), None),
            P(("fsdp", "seq"), None),
            P(("fsdp", "seq"), None),
            P(("fsdp", "seq")),
            P(("fsdp", "seq")),
            P(("fsdp", "seq"), None),
            P("fsdp", None, "seq"),
            P("fsdp", "seq", None),
            P("fsdp", "seq", None),
        ),
        out_specs=(
            P("fsdp", "seq", None),
            P("fsdp", "seq", None),
            P(("fsdp", "seq")),
            P(("fsdp", "seq")),
            P("fsdp", "seq"),
            P("fsdp", "seq"),
            P("fsdp", "seq"),
            P("seq", "fsdp"),
            P(("fsdp", "seq")),
            P(("fsdp", "seq")),
            P(("fsdp", "seq"), None),
            P("fsdp", None, "seq"),
            P("fsdp", "seq", None),
        ),
        check_vma=False,
    )
```

```python
import functools

import jax
import jax.numpy as jnp
from jax import lax
from jax.experimental import pallas as pl
from jax.experimental.pallas import tpu as pltpu
from jax.sharding import PartitionSpec as P

D = 768
HEAD_DIM = 64
EXPERTS = 32
TOP = 2
CAP = 10


EPS = 1e-06
TANH_SCALE = 0.7978845608028654
CUBIC = 0.044715


def matmul(left_side, right_side):
    return jnp.dot(left_side, right_side, preferred_element_type=jnp.float32)


def matmul_t(left_side, right_side):
    return lax.dot_general(
        left_side, right_side, (((1,), (1,)), ((), ())), preferred_element_type=jnp.float32
    )


def t_matmul(left_side, right_side):
    return lax.dot_general(
        left_side, right_side, (((0,), (0,)), ((), ())), preferred_element_type=jnp.float32
    )


def norm_forward(values):
    centre = values - jnp.mean(values, -1, keepdims=True)
    inverse = lax.rsqrt(jnp.mean(centre * centre, -1, keepdims=True) + EPS)
    return (centre * inverse, inverse)


def norm_backward(grad_normed, normed, inverse):
    return inverse * (
        grad_normed
        - jnp.mean(grad_normed, -1, keepdims=True)
        - normed * jnp.mean(grad_normed * normed, -1, keepdims=True)
    )


def gelu_both(inner_act):
    square = inner_act * inner_act
    bent = jnp.tanh(TANH_SCALE * inner_act * (1.0 + CUBIC * square))
    value = 0.5 * inner_act * (1.0 + bent)
    slope = 0.5 * (1.0 + bent) + 0.5 * inner_act * (1.0 - bent * bent) * TANH_SCALE * (
        1.0 + 3.0 * CUBIC * square
    )
    return (value, slope)


SCALING = HEAD_DIM ** (-0.5)
MIB = 1024 * 1024
WHOLE = pl.BlockSpec(memory_space=pltpu.VMEM)


def call(kernel, outputs, operands, after=(), fresh=(), scalars=(), scratch=(), flops=0, mib=20, light=False):
    moved = 0 if light else sum(v.size * v.dtype.itemsize for v in operands)
    used = len(operands)

    def inner(*refs):
        kernel(*refs[:used], *refs[used + len(after) :])

    operands = [
        operand if index in fresh or index in scalars else in_hbm([operand])[0]
        for index, operand in enumerate(operands)
    ] + in_hbm(after)
    return pl.pallas_call(
        inner,
        out_shape=outputs,
        in_specs=[
            pl.BlockSpec(memory_space=pltpu.SMEM) if index in scalars else WHOLE
            for index in range(used)
        ]
        + [pl.BlockSpec(memory_space=pl.ANY)] * len(after),
        out_specs=[WHOLE] * len(outputs),
        scratch_shapes=scratch,
        cost_estimate=pl.CostEstimate(flops=flops, bytes_accessed=moved, transcendentals=0),
        compiler_params=pltpu.CompilerParams(vmem_limit_bytes=mib * MIB),
    )(*operands)


def shaped(dtype, *shape):
    return pltpu.HBM(shape, dtype)


def in_hbm(operands):
    return [pltpu.with_memory_space_constraint(operand, pltpu.HBM) for operand in operands]


def first_norm_kernel(tokens, normed_ref):
    normed_ref[...] = norm_forward(tokens[...])[0].astype(jnp.bfloat16)


def attend_kernel(
    own, far, near, diag, held_own, held_other, parity,
    normed_ref, normed_in_ref, qkv_ref, mixed_ref, logsum_ref, vec_ref, held_ref, router_ref
):
    bf16 = jnp.bfloat16
    f32 = jnp.float32
    columns = qkv_ref.shape[1]
    outer, _, rows, lanes = held_ref.shape
    bit = parity[0]
    for place in range(outer):
        held_ref[place, bit] = held_own[place]
        held_ref[place, 1 - bit] = held_other[place]
    held = held_ref[...].reshape(outer * 2 * rows, lanes)
    wanted = lax.broadcasted_iota(jnp.int32, (8, lanes), 0) + (columns + EXPERTS)
    picker = (lax.broadcasted_iota(jnp.int32, (8, lanes), 1) == wanted).astype(bf16)
    router_ref[...] = held[:, columns : columns + EXPERTS]
    vectors = matmul_t(picker, held)
    vec_ref[...] = vectors
    count = own.shape[0]
    for index, block in enumerate((own, far, near, diag)):
        normed = block[...].astype(f32)
        rows = pl.ds(index * count, count)
        normed_ref[rows, :] = block[...]
        normed_in_ref[rows, :] = (normed * vectors[0:1] + vectors[1:2]).astype(bf16)
    qkv_ref[...] = matmul(normed_in_ref[...], held[:, :columns]).astype(bf16)
    width = columns // 3
    logsum_ref[...] = jnp.zeros_like(logsum_ref)
    for low in range(0, width, HEAD_DIM):
        query = qkv_ref[:, low : low + HEAD_DIM]
        key = qkv_ref[:, width + low : width + low + HEAD_DIM]
        value = qkv_ref[:, 2 * width + low : 2 * width + low + HEAD_DIM]
        scores = matmul_t(query, key) * SCALING
        highest = jnp.max(scores, -1, keepdims=True)
        raised = jnp.exp(scores - highest)
        total = jnp.sum(raised, -1, keepdims=True)
        head = low // HEAD_DIM
        logsum_ref[:, head : head + 1] = highest + jnp.log(total)
        weights = (raised * (1.0 / total)).astype(bf16)
        mixed_ref[:, low : low + HEAD_DIM] = matmul(weights, value).astype(bf16)


def attend_back_kernel(
    own,
    far,
    near,
    diag,
    w_out,
    held,
    qkv,
    mixed,
    logsum,
    normed,
    normed_in,
    small,
    gn_own,
    gn_far,
    gn_near,
    gn_diag,
    dw_ref,
    gr_ref,
    gqkv_ref,
):
    bf16 = jnp.bfloat16
    f32 = jnp.float32
    count = own.shape[0]
    columns = qkv.shape[1]
    width = columns // 3
    for index, block in enumerate((own, far, near, diag)):
        gr_ref[pl.ds(index * count, count), :] = block[...]
    grad_mixed = matmul_t(gr_ref[...], w_out[...]).astype(bf16)
    for low in range(0, width, HEAD_DIM):
        head = low // HEAD_DIM
        query = qkv[:, low : low + HEAD_DIM]
        key = qkv[:, width + low : width + low + HEAD_DIM]
        value = qkv[:, 2 * width + low : 2 * width + low + HEAD_DIM]
        grad_head = grad_mixed[:, low : low + HEAD_DIM]
        delta = jnp.sum(
            grad_head.astype(f32) * mixed[:, low : low + HEAD_DIM].astype(f32), -1, keepdims=True
        )
        probs = jnp.exp(matmul_t(query, key) * SCALING - logsum[:, head : head + 1])
        grad_probs = matmul_t(grad_head, value)
        grad_scores = (probs * (grad_probs - delta) * SCALING).astype(bf16)
        gqkv_ref[:, low : low + HEAD_DIM] = matmul(grad_scores, key).astype(bf16)
        gqkv_ref[:, width + low : width + low + HEAD_DIM] = t_matmul(grad_scores, query).astype(
            bf16
        )
        gqkv_ref[:, 2 * width + low : 2 * width + low + HEAD_DIM] = t_matmul(
            probs.astype(bf16), grad_head
        ).astype(bf16)
    grad_normed = matmul_t(gqkv_ref[...], held[:, :columns])
    for index, block in enumerate((gn_own, gn_far, gn_near, gn_diag)):
        block[...] = grad_normed[index * count : (index + 1) * count].astype(bf16)
    dw_ref[:, :columns] = t_matmul(normed_in[...], gqkv_ref[...]).astype(bf16)
    dw_ref[:, columns : columns + width] = t_matmul(gr_ref[...], mixed[...]).astype(bf16)
    gain_row = jnp.sum(grad_normed * normed[...].astype(f32), 0, keepdims=True)
    bias_row = jnp.sum(grad_normed, 0, keepdims=True)
    row = lax.broadcasted_iota(jnp.int32, (8, gain_row.shape[1]), 0)
    both = jnp.where(row == 0, gain_row, jnp.where(row == 1, bias_row, 0.0))
    sums = small[...] + columns_of(both, EXPERTS, small.shape[1])
    high = sums.astype(bf16)
    low = columns + width
    dw_ref[:, low:] = jnp.zeros((dw_ref.shape[0], dw_ref.shape[1] - low), bf16)
    dw_ref[:, low : low + sums.shape[1]] = high
    dw_ref[:, low + HEAD_DIM : low + HEAD_DIM + sums.shape[1]] = (
        sums - high.astype(f32)
    ).astype(bf16)


def columns_of(rows, first, lanes):
    count = rows.shape[0]
    spots = lax.broadcasted_iota(jnp.int32, (count, lanes), 1)
    placed = (spots == lax.broadcasted_iota(jnp.int32, (count, lanes), 0) + first).astype(
        jnp.float32
    )
    return lax.dot_general(
        rows,
        placed,
        (((0,), (0,)), ((), ())),
        preferred_element_type=jnp.float32,
        precision=lax.Precision.HIGHEST,
    )


def picks_of(position, choice, rows, copies):
    spots = lax.broadcasted_iota(jnp.int32, (position.shape[0], rows), 1)
    first = position[:, choice : choice + 1]
    hit = spots == first
    for copy in range(1, copies):
        hit = hit | (spots == first + copy * CAP)
    return hit.astype(jnp.float32)


def gates_of(probs, chosen, choice):
    spots = lax.broadcasted_iota(jnp.int32, probs.shape, 1)
    return jnp.sum(
        jnp.where(spots == chosen[:, choice : choice + 1], probs, 0.0), -1, keepdims=True
    )


def route_kernel(
    tokens_in, own, near, far, vectors, router, position, residual_ref, rows_ref, probs_ref, table_ref,
    *, copies
):
    bf16 = jnp.bfloat16
    f32 = jnp.float32
    residual = tokens_in[...] + (
        own[...].astype(f32) + near[...].astype(f32) + far[...].astype(f32)
    )
    residual_ref[...] = residual
    normed, _ = norm_forward(residual)
    rows = (normed * vectors[2:3, :] + vectors[3:4, :]).astype(bf16)
    rows_ref[...] = rows
    logits = matmul(rows, router[...])
    raised = jnp.exp(logits - jnp.max(logits, -1, keepdims=True))
    probs_ref[...] = raised / jnp.sum(raised, -1, keepdims=True)
    size = table_ref.shape[0]
    spots = picks_of(position[...], 0, size, copies) + picks_of(position[...], 1, size, copies)
    table_ref[...] = t_matmul(spots.astype(bf16), rows).astype(bf16)


def combine_kernel(
    residual, upstream, vectors, router, rows, probs, chosen, position, route_dots, table,
    own, near, far, regroup,
    grad_ref, half_ref, small_ref, settled_ref, *, copies
):
    bf16 = jnp.bfloat16
    f32 = jnp.float32
    size = table.shape[0]
    picks = [picks_of(position[...], choice, size, copies) for choice in range(TOP)]
    grad_probs = jnp.zeros(probs.shape, f32)
    spots = lax.broadcasted_iota(jnp.int32, probs.shape, 1)
    for choice in range(TOP):
        grad_gate = jnp.sum(picks[choice] * route_dots[0:1, :], -1, keepdims=True)
        grad_probs = grad_probs + jnp.where(
            spots == chosen[:, choice : choice + 1], grad_gate, 0.0
        )
    shares = probs[...]
    grad_logits = shares * (grad_probs - jnp.sum(shares * grad_probs, -1, keepdims=True))
    grad_logits = grad_logits.astype(bf16)
    grad_rows = matmul((picks[0] + picks[1]).astype(bf16), table[...]) + matmul_t(
        grad_logits, router[...]
    )
    normed, inverse = norm_forward(residual[...])
    grad = upstream[...] + norm_backward(grad_rows * vectors[2:3, :], normed, inverse)
    grad_ref[...] = grad
    half_ref[...] = grad.astype(bf16)
    gain_row = jnp.sum(grad_rows * normed, 0, keepdims=True)
    bias_row = jnp.sum(grad_rows, 0, keepdims=True)
    row = lax.broadcasted_iota(jnp.int32, (8, gain_row.shape[1]), 0)
    both = jnp.where(row == 0, gain_row, jnp.where(row == 1, bias_row, 0.0))
    lanes = small_ref.shape[1]
    small_ref[...] = columns_of(both, EXPERTS + 2, lanes)
    small_ref[:, :EXPERTS] = t_matmul(rows[...], grad_logits)
    settle_kernel(own, near, far, regroup, settled_ref)


def block_out_kernel(residual, probs, chosen, position, table, out_ref, *, copies):
    out = residual[...]
    for choice in range(TOP):
        pick = picks_of(position[...], choice, table.shape[0], copies).astype(jnp.bfloat16)
        out = out + gates_of(probs[...], chosen, choice) * matmul(pick, table[...])
    out_ref[...] = out


def expert_kernel(
    first,
    x_own, x_far, x_near, x_diag,
    c_own, c_far, c_near, c_diag,
    router, w_in, w_out,
    o_own, o_far, o_near, o_diag,
    g_own, g_far, g_near, g_diag,
    rows_ref, cots_ref, hidden_ref, inner_ref, dots_ref,
):
    bf16 = jnp.bfloat16
    f32 = jnp.float32
    count = x_own.shape[1]
    parts = [pl.ds(index * count, count) for index in range(4)]
    for part, block, cots in zip(
        parts, (x_own, x_far, x_near, x_diag), (c_own, c_far, c_near, c_diag)
    ):
        rows_ref[0, part, :] = block[0]
        cots_ref[0, part, :] = cots[0]
    rows = rows_ref[0]
    bare = cots_ref[0]
    logits = matmul(rows, router[...])
    raised = jnp.exp(logits - jnp.max(logits, -1, keepdims=True))
    wanted = first[0] + pl.program_id(0)
    spots = lax.broadcasted_iota(jnp.int32, logits.shape, 1)
    gate = jnp.sum(jnp.where(spots == wanted, raised, 0.0), -1, keepdims=True) / jnp.sum(
        raised, -1, keepdims=True
    )
    cots = (gate * bare.astype(f32)).astype(bf16)
    cots_ref[0] = cots
    out_sum = None
    for half in range(w_in.shape[0]):
        value, slope = gelu_both(matmul(rows, w_in[half]))
        hidden = value.astype(bf16)
        hidden_ref[half] = hidden
        inner = (matmul_t(cots, w_out[half]) * slope).astype(bf16)
        inner_ref[half] = inner
        out = matmul(hidden, w_out[half])
        grad = matmul_t(inner, w_in[half])
        out_sum = out if out_sum is None else out_sum + out
        grad_sum = grad if half == 0 else grad_sum + grad
    dots = jnp.sum(out_sum * bare.astype(f32), -1, keepdims=True)
    dots_ref[0] = jnp.broadcast_to(dots, dots_ref.shape[1:])
    for index, (out, grad) in enumerate(
        zip((o_own, o_far, o_near, o_diag), (g_own, g_far, g_near, g_diag))
    ):
        low = index * count
        out[0] = out_sum[low : low + count].astype(bf16)
        grad[0] = grad_sum[low : low + count].astype(bf16)


def experts(first, rows, cots, router, w_in, w_out):
    bf16 = jnp.bfloat16
    f32 = jnp.float32
    local_experts, count, _ = rows[0].shape
    slices, _, hidden_cols = w_in.shape
    halves = slices // local_experts
    total = 4 * count
    by_expert = pl.BlockSpec((1, count, D), lambda e: (e, 0, 0))
    by_expert_all = pl.BlockSpec((1, total, D), lambda e: (e, 0, 0))
    by_slice = lambda *shape: pl.BlockSpec((halves,) + shape, lambda e: (e, 0, 0))
    flops = 8 * slices * total * D * hidden_cols
    moved = 4 * slices * D * hidden_cols + 12 * local_experts * total * D
    return pl.pallas_call(
        expert_kernel,
        grid=(local_experts,),
        in_specs=[pl.BlockSpec(memory_space=pltpu.SMEM)]
        + [by_expert] * 8
        + [
            pl.BlockSpec((D, EXPERTS), lambda e: (0, 0)),
            by_slice(D, hidden_cols),
            by_slice(hidden_cols, D),
        ],
        out_specs=[by_expert] * 8
        + [
            by_expert_all,
            by_expert_all,
            by_slice(total, hidden_cols),
            by_slice(total, hidden_cols),
            pl.BlockSpec((1, total, 8), lambda e: (e, 0, 0)),
        ],
        out_shape=[shaped(bf16, local_experts, count, D)] * 8
        + [shaped(bf16, local_experts, total, D)] * 2
        + [shaped(bf16, slices, total, hidden_cols)] * 2
        + [shaped(f32, local_experts, total, 8)],
        cost_estimate=pl.CostEstimate(flops=flops, bytes_accessed=moved, transcendentals=0),
        compiler_params=pltpu.CompilerParams(
            vmem_limit_bytes=(28 if count <= 128 else 58) * MIB
        ),
    )(first, *rows, *cots, router, *in_hbm([w_in, w_out]))


def product_kernel(left, right, *rest):
    out_ref = rest[-1]
    for index in range(out_ref.shape[0]):
        out_ref[index] = t_matmul(
            left[min(index, left.shape[0] - 1)], right[min(index, right.shape[0] - 1)]
        )


def expert_products(left, right, after=()):
    slices = max(left.shape[0], right.shape[0])
    local_experts = min(left.shape[0], right.shape[0])
    shape = (left.shape[2], right.shape[2])
    block = lambda first, *rest: pl.BlockSpec((first // local_experts,) + rest, lambda e: (e, 0, 0))
    flops = 2 * slices * left.shape[1] * shape[0] * shape[1]
    return pl.pallas_call(
        product_kernel,
        grid=(local_experts,),
        in_specs=[block(*left.shape), block(*right.shape)]
        + [pl.BlockSpec(memory_space=pl.ANY)] * len(after),
        out_specs=block(slices, *shape),
        out_shape=shaped(jnp.float32, slices, *shape),
        cost_estimate=pl.CostEstimate(
            flops=flops,
            bytes_accessed=4 * slices * shape[0] * shape[1] + 2 * (left.size + right.size),
            transcendentals=0,
        ),
        compiler_params=pltpu.CompilerParams(
            vmem_limit_bytes=(16 if left.shape[1] <= 512 else 48) * MIB
        ),
    )(*in_hbm([left, right, *after]))


def settle_kernel(own, near, far, regroup, out_ref):
    f32 = jnp.float32
    summed = own[...].astype(f32) + near[...].astype(f32) + far[...].astype(f32)
    out_ref[...] = t_matmul(regroup[...], summed.astype(jnp.bfloat16)).astype(jnp.bfloat16)


def finish_kernel(received, query_ref, key_ref, value_ref, output_ref, small_ref):
    f32 = jnp.float32
    width = query_ref.shape[1]
    total = received[0].astype(f32)
    for index in range(1, received.shape[0]):
        total = total + received[index].astype(f32)
    query_ref[...] = total[:, :width]
    key_ref[...] = total[:, width : 2 * width]
    value_ref[...] = total[:, 2 * width : 3 * width]
    output_ref[...] = total[:, 3 * width : 4 * width].T
    low = 4 * width
    lanes = small_ref.shape[1]
    small_ref[...] = (
        total[:, low : low + lanes] + total[:, low + HEAD_DIM : low + HEAD_DIM + lanes]
    )


def weight_blocks_kernel(query, key, value, router, gain1, bias1, gain2, bias2, out_ref):
    bf16 = jnp.bfloat16
    devices_on, seq_size, shard, lanes = out_ref.shape
    width = query.shape[1] // seq_size
    spots = lax.broadcasted_iota(jnp.int32, (8, shard), 0)
    vectors = jnp.zeros((8, shard), bf16)
    for index, vector in enumerate((gain1, bias1, gain2, bias2)):
        vectors = jnp.where(spots == index, vector[...], vectors)
    tail = lanes - 3 * width
    where_to = lax.broadcasted_iota(jnp.int32, (8, tail), 0) + EXPERTS
    placed = (lax.broadcasted_iota(jnp.int32, (8, tail), 1) == where_to).astype(bf16)
    rest = t_matmul(vectors, placed).astype(bf16)
    for part in range(seq_size):
        low = part * width
        for index, matrix in enumerate((query, key, value)):
            block = matrix[:, low : low + width]
            for copy in range(devices_on):
                out_ref[copy, part, :, index * width : (index + 1) * width] = block
        for copy in range(devices_on):
            out_ref[copy, part, :, 3 * width :] = rest
            out_ref[copy, part, :, 3 * width : 3 * width + EXPERTS] = router[...]


FAR = [(index, index ^ 2) for index in range(4)]
NEAR = [(index, index ^ 1) for index in range(4)]
ACROSS = [(index, index ^ 3) for index in range(4)]


def seq_gather(block):
    far = lax.ppermute(block, "seq", FAR)
    return (block, far, lax.ppermute(block, "seq", NEAR), lax.ppermute(far, "seq", NEAR))


def seq_reduce(own, far, near, diag):
    beside = lax.ppermute(diag, "seq", NEAR)
    pair = (far.astype(jnp.float32) + beside.astype(jnp.float32)).astype(far.dtype)
    return (own, lax.ppermute(near, "seq", NEAR), lax.ppermute(pair, "seq", FAR))


def body(
    block_in,
    expert_ids,
    ln1_gain,
    ln1_bias,
    w_query,
    w_key,
    w_value,
    w_output,
    ln2_gain,
    ln2_bias,
    w_router,
    w_expert_in,
    w_expert_out,
    cotangent,
):
    bf16 = jnp.bfloat16
    f32 = jnp.float32
    fsdp_size = lax.axis_size("fsdp")
    seq_size = lax.axis_size("seq")
    devices = fsdp_size * seq_size
    shard = w_query.shape[0]
    head_cols = D // seq_size
    local_slices = w_expert_in.shape[0]
    local_experts = max(1, local_slices // 2)
    halves = local_slices // local_experts
    copies = 2 // halves
    tokens_in = block_in[0]
    upstream = cotangent[0]
    chosen = expert_ids[0]
    token_count = chosen.shape[0]

    moves = [
        (fsdp_size * part + place, seq_size * place + part)
        for part in range(seq_size)
        for place in range(fsdp_size)
    ]
    w_out_rows = lax.ppermute(w_output, ("fsdp", "seq"), moves)
    w_out_rows = jnp.broadcast_to(w_out_rows, (fsdp_size, shard, D))
    w_out_rows = lax.all_to_all(w_out_rows, "fsdp", split_axis=0, concat_axis=0, tiled=True)
    w_out_rows = w_out_rows.reshape(head_cols, D)
    lanes = 3 * head_cols + EXPERTS + 4
    outer = fsdp_size // 2
    parity = lax.axis_index("fsdp") % 2
    sent = call(
        weight_blocks_kernel,
        [shaped(bf16, outer, seq_size, shard, lanes)],
        [w_query, w_key, w_value, w_router]
        + [v.reshape(1, shard) for v in (ln1_gain, ln1_bias, ln2_gain, ln2_bias)],
    )[0].reshape(devices // 2, shard, -1)
    groups = [
        [(2 * place + bit) * seq_size + part for place in range(outer) for part in range(seq_size)]
        for bit in range(2)
    ]
    held_own = lax.all_to_all(
        sent,
        ("fsdp", "seq"),
        split_axis=0,
        concat_axis=0,
        axis_index_groups=groups,
        tiled=True,
    )
    image_rows = seq_size * shard
    held_own = held_own.reshape(outer, image_rows, lanes)
    held_other = lax.ppermute(held_own, "fsdp", [(i, i ^ 1) for i in range(fsdp_size)])
    if image_rows % 16:
        pairs = jnp.stack([held_own, held_other], 1)
        pairs = jnp.where(parity == 0, pairs, pairs[:, ::-1]).reshape(2, 1, D // 2, lanes)
        held_own, held_other = pairs[0], pairs[1]
        parity = jnp.zeros((), jnp.int32)
    parity = parity.astype(jnp.int32).reshape(1)

    hot = (chosen.reshape(-1)[:, None] == jnp.arange(EXPERTS)[None, :]).astype(bf16)
    routes = token_count * TOP
    earlier = (jnp.arange(routes)[:, None] > jnp.arange(routes)[None, :]).astype(bf16)
    slot = jnp.sum(matmul(earlier, hot) * hot.astype(f32), 1).astype(jnp.int32)
    position = chosen * (CAP * copies) + slot.reshape(token_count, TOP)
    table_rows = EXPERTS * copies * CAP
    local_rows = local_experts * fsdp_size * CAP
    spot = jnp.arange(local_rows)
    source_of = (spot // CAP % fsdp_size) * (local_experts * CAP) + (
        spot // (CAP * fsdp_size) * CAP + spot % CAP
    )
    regroup = (source_of[:, None] == spot[None, :]).astype(bf16)

    def to_experts(table):
        table = table.reshape(fsdp_size, local_experts * CAP, D)
        received = lax.all_to_all(table, "fsdp", split_axis=0, concat_axis=0, tiled=True)
        grouped = matmul(regroup, received.reshape(local_rows, D)).astype(bf16)
        return seq_gather(grouped.reshape(local_experts, fsdp_size * CAP, D))

    def settle(partial, after):
        blocks = [part.reshape(local_rows, D) for part in seq_reduce(*partial)]
        return call(
            settle_kernel,
            [shaped(bf16, local_rows, D)],
            [*blocks, regroup],
            after=after,
            fresh=(1, 2),
            flops=2 * local_rows * local_rows * D,
        )[0]

    def from_experts(settled):
        returned = lax.all_to_all(
            settled.reshape(fsdp_size, local_experts * CAP, D),
            "fsdp",
            split_axis=0,
            concat_axis=0,
            tiled=True,
        )
        return returned.reshape(table_rows, D)

    normed_blocks = seq_gather(
        call(first_norm_kernel, [shaped(bf16, token_count, D)], [tokens_in])[0]
    )
    image = token_count * seq_size
    columns = 3 * head_cols
    normed_one, normed_in, qkv, head_mixed, logsum, vectors, held, router = call(
        attend_kernel,
        [
            shaped(bf16, image, D),
            shaped(bf16, image, D),
            shaped(bf16, image, columns),
            shaped(bf16, image, head_cols),
            shaped(f32, image, 8),
            shaped(f32, 8, D),
            shaped(bf16, held_own.shape[0], 2, *held_own.shape[1:]),
            shaped(bf16, D, EXPERTS),
        ],
        [*normed_blocks, held_own, held_other, parity],
        fresh=(1, 2, 3, 4, 5),
        scalars=(6,),
        flops=3 * (2 * image * D * columns + 4 * image * image * head_cols),
    )
    held = held.reshape(D, lanes)
    out_partial = matmul(head_mixed, w_out_rows).astype(bf16)
    out_blocks = [out_partial[i * token_count : (i + 1) * token_count] for i in range(seq_size)]

    residual, expert_rows, router_probs, rows_table = call(
        functools.partial(route_kernel, copies=copies),
        [
            shaped(f32, token_count, D),
            shaped(bf16, token_count, D),
            shaped(f32, token_count, EXPERTS),
            shaped(bf16, table_rows, D),
        ],
        [tokens_in, *seq_reduce(*out_blocks), vectors, router, position],
        fresh=(1, 2, 3, 6),
        light=True,
    )
    spots = jnp.arange(table_rows)[None, None, :] - position[:, :, None]
    hits = (spots == 0) if copies == 1 else ((spots == 0) | (spots == CAP))
    cots_table = t_matmul(jnp.any(hits, 1).astype(bf16), upstream.astype(bf16)).astype(bf16)
    slot_cots = to_experts(cots_table)
    slot_rows = to_experts(rows_table)

    first = (lax.axis_index("fsdp") * local_slices // 2).astype(jnp.int32).reshape(1)
    results = experts(
        first,
        slot_rows,
        slot_cots,
        router,
        w_expert_in,
        w_expert_out,
    )
    out_parts, grad_parts = results[:4], results[4:8]
    all_rows, all_cots, hidden_act, grad_inner, dots = results[8:]
    me = lax.axis_index("seq")
    turned = jnp.array([0, 2, 1, 3])[me ^ jnp.arange(seq_size)]
    dots = dots[:, :, 0].reshape(local_experts, seq_size, fsdp_size, CAP)
    dots = jnp.take(dots.transpose(2, 1, 0, 3), turned, axis=1)
    dots = lax.all_to_all(
        dots.reshape(devices, 1, local_experts * CAP),
        ("fsdp", "seq"),
        split_axis=0,
        concat_axis=0,
        tiled=True,
    )
    route_dots = jnp.sum(dots.reshape(fsdp_size, seq_size, -1), 1).reshape(1, table_rows)
    grad_table = from_experts(settle(grad_parts, []))
    grad_residual, grad_res_half, small_sums, out_settled = call(
        functools.partial(combine_kernel, copies=copies),
        [
            shaped(f32, token_count, D),
            shaped(bf16, token_count, D),
            shaped(f32, D, EXPERTS + 4),
            shaped(bf16, local_rows, D),
        ],
        [
            residual,
            upstream,
            vectors,
            router,
            expert_rows,
            router_probs,
            chosen,
            position,
            route_dots,
            grad_table,
            *[block.reshape(local_rows, D) for block in seq_reduce(*out_parts)],
            regroup,
        ],
        fresh=(6, 7, 8, 9, 11, 12),
    )

    out_table = from_experts(out_settled)
    block_out = call(
        functools.partial(block_out_kernel, copies=copies),
        [shaped(f32, token_count, D)],
        [residual, router_probs, chosen, position, out_table],
        fresh=(2, 3, 4),
    )[0]

    *gn_parts, grad_weights = call(
        attend_back_kernel,
        [shaped(bf16, token_count, D)] * 4
        + [shaped(bf16, D, 4 * head_cols + 2 * HEAD_DIM)],
        [
            *seq_gather(grad_res_half),
            w_out_rows,
            held,
            qkv,
            head_mixed,
            logsum,
            normed_one,
            normed_in,
            small_sums,
        ],
        fresh=(1, 2, 3, 4),
        scratch=[pltpu.VMEM((image, D), bf16), pltpu.VMEM((image, columns), bf16)],
        flops=4 * (4 * image * D * 4 * head_cols + 10 * image * image * head_cols),
    )
    grad_weights = lax.all_to_all(
        grad_weights.reshape(fsdp_size, D // fsdp_size, 4 * head_cols + 2 * HEAD_DIM),
        "fsdp",
        split_axis=0,
        concat_axis=0,
        tiled=True,
    )
    own, near, far = seq_reduce(*gn_parts)
    grad_expert_in = expert_products(all_rows, grad_inner, [far])
    grad_expert_out = expert_products(hidden_act, all_cots, [far])
    *grad_squares, small_sums = call(
        finish_kernel,
        [shaped(f32, D // fsdp_size, head_cols)] * 3
        + [shaped(f32, head_cols, D // fsdp_size), shaped(f32, D // fsdp_size, EXPERTS + 4)],
        [grad_weights],
        after=[block_out, grad_expert_in, grad_expert_out],
        fresh=(0,),
    )
    pieces = []
    for step, swap in ((0, None), (2, FAR), (1, NEAR), (3, ACROSS)):
        piece = lax.dynamic_slice_in_dim(small_sums, (me ^ step) * shard, shard)
        pieces.append(piece if swap is None else lax.ppermute(piece, "seq", swap))
    small_sums = (pieces[0] + pieces[1]) + (pieces[2] + pieces[3])
    own_grad_normed = own.astype(f32) + near.astype(f32) + far.astype(f32)
    own_normed, own_inverse = norm_forward(tokens_in)
    grad_tokens = grad_residual + norm_backward(
        own_grad_normed * vectors[0], own_normed, own_inverse
    )
    return (
        block_out[None],
        grad_tokens[None],
        small_sums[:, EXPERTS],
        small_sums[:, EXPERTS + 1],
        *grad_squares,
        small_sums[:, EXPERTS + 2],
        small_sums[:, EXPERTS + 3],
        small_sums[:, :EXPERTS],
        grad_expert_in,
        grad_expert_out,
    )


def solution(mesh):
    return jax.shard_map(
        body,
        mesh=mesh,
        in_specs=(
            P("fsdp", "seq", None),
            P("fsdp", "seq", None),
            P(("fsdp", "seq")),
            P(("fsdp", "seq")),
            P(("fsdp", "seq"), None),
            P(("fsdp", "seq"), None),
            P(("fsdp", "seq"), None),
            P(("fsdp", "seq"), None),
            P(("fsdp", "seq")),
            P(("fsdp", "seq")),
            P(("fsdp", "seq"), None),
            P("fsdp", None, "seq"),
            P("fsdp", "seq", None),
            P("fsdp", "seq", None),
        ),
        out_specs=(
            P("fsdp", "seq", None),
            P("fsdp", "seq", None),
            P(("fsdp", "seq")),
            P(("fsdp", "seq")),
            P("fsdp", "seq"),
            P("fsdp", "seq"),
            P("fsdp", "seq"),
            P("seq", "fsdp"),
            P(("fsdp", "seq")),
            P(("fsdp", "seq")),
            P(("fsdp", "seq"), None),
            P("fsdp", None, "seq"),
            P("fsdp", "seq", None),
        ),
        check_vma=False,
    )
```
